128 devices in a mesh: func: 128 (over z, x, y, core).
Axes of the slice: x: 4, y: 4, z: 4, core: 2. Of those that a mesh axis runs over, the one named last changes fastest.
Arguments:
- basis_wavefunctions: bfloat16 [16384, 8, 2048], P('func')
- filling_weights: float32 [16384], P('func'), may hold values from 0.5 to 2
- living_per_unit: int32 [128], replicated, may hold values from 64 to 128, as said below
- starting_sheets: int32 [16384], replicated, may hold values from 0 to 1023, as said below
- nucleus_charge: float32 [1024, 2048], P('func'), may hold values from 0.2 to 2
- applied_field: float32 [1024, 2048], P('func'), may hold values from -2 to 2
Outputs:
- charge_distribution: float32 [1024, 2048], P('func')
- ham: float32 [16384, 384], P('func')
- ovl: float32 [16384, 384], P('func')
The draws below stay inside these ranges and needn't reach their ends.
Inputs may be any that keep to these rules, and one draw needn't show every extreme that they name: `living_per_unit`: one device holds exactly 128 live functions. `starting_sheets`: slot s of device k starts at plane k * 8 + t with 0 <= t < 8; slot 0 has t = 0 and slot 127 has t = 7.
All inputs are finite; a program needn't handle non-finite values.
Results may differ from the reference program's by a relative error of at most 0.0003.
Values may be sent and summed in bfloat16 or wider, within the bound.
A program may use at most 192 MiB of HBM per device.

```python
import math
import jax
import jax.numpy as jnp
from jax import lax

SLAB = 8
SHEET_POINTS = 2048
F_MAX = 128
LATTICE_SHEETS = 1024
NF = 16384
N_FUNC = 128


def draw_basis_wavefunctions(key, part):
    key = jax.random.fold_in(key, 11)
    mean_key, noise_key = jax.random.split(key)
    array_shape = (N_FUNC * F_MAX, SLAB, SHEET_POINTS)
    level = jax.random.uniform(mean_key, (N_FUNC * F_MAX, 1, 1), jnp.float32, 0.5, 1.5)
    noise = jax.random.normal(noise_key, array_shape, jnp.float32)
    return (level + noise).astype(jnp.bfloat16)


def draw_living_per_unit(key, part):
    key = jax.random.fold_in(key, 23)
    first, second = jax.random.split(key)
    drawn = jax.random.randint(first, (N_FUNC,), F_MAX // 2, F_MAX + 1)
    chosen = jax.random.randint(second, (), 0, N_FUNC)
    return jnp.where(jnp.arange(N_FUNC) == chosen, F_MAX, drawn).astype(jnp.int32)


def draw_starting_sheets(key, part):
    key = jax.random.fold_in(key, 37)
    slots = jnp.arange(N_FUNC * F_MAX, dtype=jnp.int32)
    inner = jax.random.randint(key, (N_FUNC * F_MAX,), 0, SLAB)
    within = slots % F_MAX
    inner = jnp.where(within == 0, 0, jnp.where(within == F_MAX - 1, SLAB - 1, inner))
    return (slots // F_MAX * SLAB + inner).astype(jnp.int32)


def steps_of(stream_key, dims, shards, smallest, top_value):
    level, own = 1.0, jax.random.fold_in(stream_key, 6)
    for position, parts in shards:
        draws = jnp.exp(jax.random.uniform(jax.random.fold_in(own, position), (parts,), jnp.float32, smallest / len(shards), top_value / len(shards)))
        level = level * jnp.repeat(draws, dims[position] // parts).reshape([-1 if axis == position else 1 for axis in range(len(dims))])
    return level


def setup_inputs(seed: int = 0) -> dict:
    key_list = jax.random.split(jax.random.key(seed), 7)
    return {
        "basis_wavefunctions": draw_basis_wavefunctions(jax.random.fold_in(key_list[6], 71), 0),
        "filling_weights": jnp.clip(jnp.exp(math.log(2.0) - 1.3862944 * jax.random.uniform(key_list[1], (NF,), jnp.float32) ** steps_of(key_list[1], (NF,), ((0, 128),), -0.2, 0.2)), 0.5, 2.0),
        "living_per_unit": draw_living_per_unit(jax.random.fold_in(key_list[6], 71), 0),
        "starting_sheets": draw_starting_sheets(jax.random.fold_in(key_list[6], 71), 0),
        "nucleus_charge": jnp.clip(jnp.exp(math.log(2.0) - 2.3025851 * jax.random.uniform(key_list[4], (LATTICE_SHEETS, SHEET_POINTS), jnp.float32) ** steps_of(key_list[4], (LATTICE_SHEETS, SHEET_POINTS), ((0, 128),), -0.2, 0.2)), 0.2, 2.0),
        "applied_field": jnp.clip(jax.random.uniform(key_list[5], (LATTICE_SHEETS, SHEET_POINTS), jnp.float32, -2.0, 2.0) * steps_of(key_list[5], (LATTICE_SHEETS, SHEET_POINTS), ((0, 128),), -0.4, 0.0), -2.0, 2.0),
    }


def reference(basis_wavefunctions, filling_weights, living_per_unit, starting_sheets, nucleus_charge, applied_field):
    nf = N_FUNC * F_MAX
    slots = jnp.arange(nf, dtype=jnp.int32)
    owner = slots // F_MAX
    active_flags = (slots % F_MAX) < living_per_unit[owner]
    support_orbitals = jnp.where(active_flags[:, None, None], basis_wavefunctions, jnp.zeros_like(basis_wavefunctions)).astype(jnp.bfloat16)
    weight = filling_weights * active_flags.astype(jnp.float32)
    charge_distribution = nucleus_charge
    for b in range(SLAB):
        plane = (starting_sheets + b) % LATTICE_SHEETS
        term = weight[:, None] * jnp.square(support_orbitals[:, b, :].astype(jnp.float32))
        charge_distribution = charge_distribution + jax.ops.segment_sum(term, plane, num_segments=LATTICE_SHEETS)
    effective_field_mesh = applied_field - 0.9847 * jnp.cbrt(charge_distribution)
    phi4 = support_orbitals.reshape(N_FUNC, F_MAX, SLAB, SHEET_POINTS)
    offs4 = starting_sheets.reshape(N_FUNC, F_MAX)
    rows = jnp.arange(2 * SLAB, dtype=jnp.int32)
    cols = jnp.arange(SLAB, dtype=jnp.int32)

    def place_dev(d):
        boxes = phi4[d].astype(jnp.float32)
        start = offs4[d] - d * SLAB
        shifter = (rows[None, :, None] == start[:, None, None] + cols[None, None, :]).astype(jnp.float32)
        placed = jnp.einsum('iwb,ibp->iwp', shifter, boxes, precision=lax.Precision.HIGHEST)
        potwin = effective_field_mesh[(d * SLAB + rows) % LATTICE_SHEETS]
        rounded = lax.optimization_barrier((potwin[None] * placed).astype(jnp.bfloat16))
        return jnp.stack([placed, rounded.astype(jnp.float32)])

    def pairs(left, right):
        return jnp.einsum('iwp,sjwp->sij', left, right, precision=lax.Precision.HIGHEST)

    def one_device(k):
        own = place_dev(k)
        prev = place_dev((k - 1) % N_FUNC)
        nxt = place_dev((k + 1) % N_FUNC)
        left = own[0]
        block_prev = pairs(left[:, :SLAB], prev[:, :, SLAB:])
        block_own = pairs(left, own)
        block_next = pairs(left[:, SLAB:], nxt[:, :, :SLAB])
        return jnp.concatenate([block_prev, block_own, block_next], axis=2) * (1.0 / (SLAB * SHEET_POINTS))

    blocks = lax.map(one_device, jnp.arange(N_FUNC, dtype=jnp.int32))
    ovl = blocks[:, 0].reshape(nf, 3 * F_MAX)
    ham = blocks[:, 1].reshape(nf, 3 * F_MAX)
    return charge_distribution, ham, ovl
```

```python
import functools

import jax
import jax.numpy as jnp
from jax import lax
from jax.experimental import pallas as pl
from jax.experimental.pallas import tpu as pltpu
from jax.sharding import PartitionSpec as P

MESH = pl.DeviceIdType.MESH
F32 = jnp.float32
BF16 = jnp.bfloat16

SLOTS = 128
DEPTH = 8
PLANES = 2 * DEPTH - 1
GROUP = 16
GROUPS = SLOTS // GROUP
PIECES = 4


def dot_nt(a, b):
    return lax.dot_general(a, b, (((1,), (1,)), ((), ())), preferred_element_type=F32)


def cube_root(x):
    y = jnp.exp(jnp.log(x) * (1.0 / 3.0))
    return (2.0 * y + x / (y * y)) * (1.0 / 3.0)


def kernel(
    count,
    boxes,
    weights,
    living,
    sheets,
    nucleus,
    applied,
    rho_out,
    ham_out,
    ovl_out,
    raw,
    selector,
    wide_weights,
    stack,
    from_prev,
    from_next,
    dens,
    pot,
    rho,
    up_out,
    up_in,
    down_out,
    down_in,
    own,
    part,
    part_in,
    ham,
    ovl,
    raw_sem,
    down_sems,
    up_sems,
    planes_down_sems,
    planes_up_sems,
    plane_sems,
    part_sems,
    out_sems,
):
    me = lax.axis_index("func")
    following = lax.rem(me + 1, count)
    preceding = lax.rem(me + count - 1, count)
    width = raw.shape[2]

    def points(piece):
        return pl.ds(pl.multiple_of(piece * width, width), width)

    def raw_copy(piece):
        return pltpu.make_async_copy(
            boxes.at[:, points(piece)], raw.at[piece], raw_sem.at[piece]
        )

    for piece in range(PIECES):
        raw_copy(piece).start()

    barrier = pltpu.get_barrier_semaphore()
    for neighbour in (preceding, following):
        pl.semaphore_signal(barrier, inc=1, device_id=(neighbour,), device_id_type=MESH)

    start = (sheets[pl.ds(me, 1), :] - me * DEPTH).astype(F32)
    lane = lax.broadcasted_iota(jnp.int32, (1, SLOTS), 1)
    start = jnp.where(lane < living[me], start, 64.0)
    lanes = lax.broadcasted_iota(jnp.int32, (GROUPS, SLOTS), 1)
    rows = lax.broadcasted_iota(jnp.int32, (GROUPS, SLOTS), 0)
    spread = jnp.where(lanes // GROUP == rows, start, 0.0).astype(BF16)
    repeat = (
        lax.broadcasted_iota(jnp.int32, (SLOTS, SLOTS), 0) % GROUP
        == lax.broadcasted_iota(jnp.int32, (SLOTS, SLOTS), 1) // DEPTH
    )
    column_start = jnp.dot(
        spread, jnp.where(repeat, 1.0, 0.0).astype(BF16), preferred_element_type=F32
    )
    row = lax.broadcasted_iota(jnp.int32, (PLANES * GROUP, SLOTS), 0)
    column = lax.broadcasted_iota(jnp.int32, (PLANES * GROUP, SLOTS), 1)
    offset = jnp.where(
        row % GROUP == column // DEPTH, row // GROUP - column % DEPTH, -99
    ).astype(F32)
    for group in range(GROUPS):
        selector[group] = jnp.where(offset == column_start[group : group + 1, :], 1.0, 0.0).astype(BF16)
    wide_weights[...] = jnp.broadcast_to(weights[...], (SLOTS, SLOTS)).T

    pl.semaphore_wait(barrier, 2)

    def down_copy(piece):
        return pltpu.make_async_remote_copy(
            src_ref=down_out.at[piece],
            dst_ref=down_in.at[piece],
            send_sem=down_sems.at[0, piece],
            recv_sem=down_sems.at[1, piece],
            device_id=(following,),
            device_id_type=MESH,
        )

    def up_copy(piece):
        return pltpu.make_async_remote_copy(
            src_ref=up_out.at[piece],
            dst_ref=up_in.at[piece],
            send_sem=up_sems.at[0, piece],
            recv_sem=up_sems.at[1, piece],
            device_id=(preceding,),
            device_id_type=MESH,
        )

    def planes_down_copy(piece):
        return pltpu.make_async_remote_copy(
            src_ref=stack.at[piece, pl.ds(DEPTH + 4, 3), pl.ds(0, SLOTS), :],
            dst_ref=from_prev.at[piece, pl.ds(1, 3)],
            send_sem=planes_down_sems.at[0, piece],
            recv_sem=planes_down_sems.at[1, piece],
            device_id=(following,),
            device_id_type=MESH,
        )

    def planes_up_copy(piece):
        return pltpu.make_async_remote_copy(
            src_ref=stack.at[piece, pl.ds(0, 3), pl.ds(0, SLOTS), :],
            dst_ref=from_next.at[piece, pl.ds(0, 3)],
            send_sem=planes_up_sems.at[0, piece],
            recv_sem=planes_up_sems.at[1, piece],
            device_id=(preceding,),
            device_id_type=MESH,
        )

    def plane_up_copy(piece):
        return pltpu.make_async_remote_copy(
            src_ref=stack.at[piece, 3, pl.ds(0, SLOTS), :],
            dst_ref=from_next.at[piece, 3],
            send_sem=plane_sems.at[0, piece],
            recv_sem=plane_sems.at[1, piece],
            device_id=(preceding,),
            device_id_type=MESH,
        )

    def plane_down_copy(piece):
        return pltpu.make_async_remote_copy(
            src_ref=stack.at[piece, DEPTH + 3, pl.ds(0, SLOTS), :],
            dst_ref=from_prev.at[piece, 0],
            send_sem=plane_sems.at[0, piece],
            recv_sem=plane_sems.at[1, piece],
            device_id=(following,),
            device_id_type=MESH,
        )

    def place_piece(piece, carry):
        raw_copy(piece).wait()
        dens[...] = jnp.zeros_like(dens)

        def place_group(group, carry):
            slots = pl.ds(pl.multiple_of(group * GROUP, GROUP), GROUP)
            source = raw[piece, pl.ds(pl.multiple_of(group * GROUP * DEPTH, GROUP * DEPTH), GROUP * DEPTH), :]
            placed = jnp.dot(selector[group], source, preferred_element_type=F32)
            placed = placed.reshape(PLANES, GROUP, width)
            stack[piece, :, slots, :] = placed.astype(BF16)
            weight = jnp.concatenate([wide_weights[slots, :]] * (width // SLOTS), axis=1)
            terms = placed * placed * weight[None]
            dens[...] += terms[:, :DEPTH] + terms[:, DEPTH:]
            return carry

        lax.fori_loop(0, GROUPS, place_group, 0)
        down_out[piece] = jnp.zeros_like(down_out[piece])
        down_out[piece, : DEPTH - 1] = jnp.sum(dens[DEPTH:], axis=1)
        up_out[piece, 0] = nucleus[:, points(piece)] + jnp.sum(dens[:DEPTH], axis=1)
        up_out[piece, 1] = applied[:, points(piece)]
        down_copy(piece).start()
        up_copy(piece).start()
        planes_down_copy(piece).start()
        planes_up_copy(piece).start()

        @pl.when(piece < PIECES // 2)
        def _():
            plane_up_copy(piece).start()

        @pl.when(piece >= PIECES // 2)
        def _():
            plane_down_copy(piece).start()

        return carry

    lax.fori_loop(0, PIECES, place_piece, 0)

    own[...] = jnp.zeros_like(own)

    def own_piece(piece, carry):
        down_copy(piece).wait()
        up_copy(piece).wait()
        density = up_out[piece, 0] + down_in[piece]
        rho[:, points(piece)] = density
        pot[piece, :DEPTH] = up_out[piece, 1] - 0.9847 * cube_root(density)
        pot[piece, DEPTH:] = up_in[piece, 1] - 0.9847 * cube_root(up_in[piece, 0] + down_out[piece])
        total = own[...]
        for plane in range(PLANES):
            phi = stack[piece, plane, :SLOTS, :]
            stack[piece, plane, SLOTS:, :] = (phi.astype(F32) * pot[piece, plane : plane + 1, :]).astype(BF16)
            total += dot_nt(phi, stack[piece, plane])
        own[...] = total
        return carry

    lax.fori_loop(0, PIECES, own_piece, 0)
    rho_copy = pltpu.make_async_copy(rho, rho_out, out_sems.at[0])
    rho_copy.start()

    scale = 1.0 / (DEPTH * width * PIECES)
    part[...] = jnp.zeros_like(part)

    def cross_piece(piece, carry):
        planes_up_copy(piece).wait()
        planes_down_copy(piece).wait()
        total = part[0]
        for shared in range(3):
            total += dot_nt(from_next[piece, shared], stack[piece, DEPTH + shared])
        part[0] = total
        total = part[1]
        for shared in range(4, 7):
            total += dot_nt(from_prev[piece, shared - 3], stack[piece, shared])
        part[1] = total

        @pl.when(piece < PIECES // 2)
        def _():
            plane_up_copy(piece).wait()
            part[0] += dot_nt(from_next[piece, 3], stack[piece, DEPTH + 3])

        @pl.when(piece >= PIECES // 2)
        def _():
            plane_down_copy(piece).wait()
            part[1] += dot_nt(from_prev[piece, 0], stack[piece, 3])

        return carry

    lax.fori_loop(0, PIECES, cross_piece, 0)

    def part_copy(side, target):
        return pltpu.make_async_remote_copy(
            src_ref=part.at[side],
            dst_ref=part_in.at[side],
            send_sem=part_sems.at[0, side],
            recv_sem=part_sems.at[1, side],
            device_id=(target,),
            device_id_type=MESH,
        )

    to_next = part_copy(0, following)
    to_prev = part_copy(1, preceding)
    to_next.start()
    to_prev.start()
    ovl[:, SLOTS : 2 * SLOTS] = own[:, :SLOTS] * scale
    ham[:, SLOTS : 2 * SLOTS] = own[:, SLOTS:] * scale
    ovl_next = part[0, :, :SLOTS].T
    ham_next = part[0, :, SLOTS:].T
    ovl_prev = part[1, :, :SLOTS].T
    ham_prev = part[1, :, SLOTS:].T
    to_next.wait()
    to_prev.wait()
    ovl[:, :SLOTS] = (ovl_prev + part_in[0, :, :SLOTS]) * scale
    ham[:, :SLOTS] = (ham_prev + part_in[0, :, SLOTS:]) * scale
    ovl[:, 2 * SLOTS :] = (ovl_next + part_in[1, :, :SLOTS]) * scale
    ham[:, 2 * SLOTS :] = (ham_next + part_in[1, :, SLOTS:]) * scale
    ovl_copy = pltpu.make_async_copy(ovl, ovl_out, out_sems.at[1])
    ham_copy = pltpu.make_async_copy(ham, ham_out, out_sems.at[2])
    ovl_copy.start()
    ham_copy.start()
    rho_copy.wait()
    ovl_copy.wait()
    ham_copy.wait()


def per_device(
    basis_wavefunctions,
    filling_weights,
    living_per_unit,
    starting_sheets,
    nucleus_charge,
    applied_field,
):
    slots, depth, points = basis_wavefunctions.shape
    count = lax.axis_size("func")
    width = points // PIECES
    vmem = pl.BlockSpec(memory_space=pltpu.VMEM)
    anywhere = pl.BlockSpec(memory_space=pl.ANY)
    pair = pltpu.SemaphoreType.DMA((2, PIECES))
    rho, ham, ovl = pl.pallas_call(
        functools.partial(kernel, count),
        out_shape=(
            jax.ShapeDtypeStruct((depth, points), F32),
            jax.ShapeDtypeStruct((slots, 3 * slots), F32),
            jax.ShapeDtypeStruct((slots, 3 * slots), F32),
        ),
        in_specs=[
            anywhere,
            vmem,
            pl.BlockSpec(memory_space=pltpu.SMEM),
            vmem,
            vmem,
            vmem,
        ],
        out_specs=(anywhere, anywhere, anywhere),
        scratch_shapes=[
            pltpu.VMEM((PIECES, slots * depth, width), BF16),
            pltpu.VMEM((GROUPS, PLANES * GROUP, slots), BF16),
            pltpu.VMEM((slots, slots), F32),
            pltpu.VMEM((PIECES, PLANES, 2 * slots, width), BF16),
            pltpu.VMEM((PIECES, 4, slots, width), BF16),
            pltpu.VMEM((PIECES, 4, slots, width), BF16),
            pltpu.VMEM((PLANES, DEPTH, width), F32),
            pltpu.VMEM((PIECES, 2 * DEPTH, width), F32),
            pltpu.VMEM((depth, points), F32),
            pltpu.VMEM((PIECES, 2, DEPTH, width), F32),
            pltpu.VMEM((PIECES, 2, DEPTH, width), F32),
            pltpu.VMEM((PIECES, DEPTH, width), F32),
            pltpu.VMEM((PIECES, DEPTH, width), F32),
            pltpu.VMEM((slots, 2 * slots), F32),
            pltpu.VMEM((2, slots, 2 * slots), F32),
            pltpu.VMEM((2, slots, 2 * slots), F32),
            pltpu.VMEM((slots, 3 * slots), F32),
            pltpu.VMEM((slots, 3 * slots), F32),
            pltpu.SemaphoreType.DMA((PIECES,)),
            pair,
            pair,
            pair,
            pair,
            pair,
            pltpu.SemaphoreType.DMA((2, 2)),
            pltpu.SemaphoreType.DMA((3,)),
        ],
        compiler_params=pltpu.CompilerParams(
            collective_id=0, has_side_effects=True, vmem_limit_bytes=56 * 2**20
        ),
        cost_estimate=pl.CostEstimate(
            flops=4 * 10**9, bytes_accessed=5 * 2**20, transcendentals=2**16
        ),
    )(
        basis_wavefunctions.reshape(slots * depth, points),
        filling_weights.reshape(1, slots),
        living_per_unit,
        starting_sheets.reshape(count, slots),
        nucleus_charge,
        applied_field,
    )
    return rho, ham, ovl


def solution(mesh):
    return jax.shard_map(
        per_device,
        mesh=mesh,
        in_specs=(P("func", None, None), P("func"), P(), P(), P("func", None), P("func", None)),
        out_specs=(P("func", None), P("func", None), P("func", None)),
        check_vma=False,
    )
```

```python
import functools

import jax
import jax.numpy as jnp
from jax import lax
from jax.experimental import pallas as pl
from jax.experimental.pallas import tpu as pltpu
from jax.sharding import PartitionSpec as P

MESH = pl.DeviceIdType.MESH
F32 = jnp.float32
BF16 = jnp.bfloat16

SLOTS = 128
DEPTH = 8
PLANES = 2 * DEPTH - 1
GROUP = 16
GROUPS = SLOTS // GROUP
PIECES = 4
LEVELS = 4
ROOM = (32, 64, 80, 96)
FIRST = (0, 32, 96, 176)
FEW, MANY = 176, 272
PARTS = 96


def dot_nt(a, b):
    return lax.dot_general(a, b, (((1,), (1,)), ((), ())), preferred_element_type=F32)


def cube_root(x):
    y = jnp.exp(jnp.log(x) * (1.0 / 3.0))
    return (2.0 * y + x / (y * y)) * (1.0 / 3.0)


def dot_nn(a, b):
    return lax.dot_general(a, b, (((1,), (0,)), ((), ())), preferred_element_type=F32)


def select_rows(one_hot, values):
    high = values.astype(BF16)
    low = (values - high.astype(F32)).astype(BF16)
    return dot_nn(one_hot, high) + dot_nn(one_hot, low)


def select_columns(values, one_hot):
    high = values.astype(BF16)
    low = (values - high.astype(F32)).astype(BF16)
    return dot_nn(high, one_hot) + dot_nn(low, one_hot)


def rank_matrix(key):
    row = lax.broadcasted_iota(jnp.int32, (SLOTS, SLOTS), 0)
    column = lax.broadcasted_iota(jnp.int32, (SLOTS, SLOTS), 1)
    wide = jnp.broadcast_to(key, (SLOTS, SLOTS))
    tall = wide.T
    before = jnp.where((tall < wide) | ((tall == wide) & (row < column)), 1.0, 0.0)
    rank = jnp.sum(before, axis=0, keepdims=True)
    return jnp.where(row.astype(F32) == rank, 1.0, 0.0)


def packed_kernel(
    count,
    boxes,
    weights_in,
    living_in,
    sheets_in,
    nucleus_in,
    applied_in,
    rho_out,
    own_out,
    side_out,
    part_in,
    back_out,
    over_out,
    raw,
    weights,
    living,
    sheets,
    nucleus,
    applied,
    starts,
    selector,
    wide_weights,
    order,
    back,
    stack,
    to_prev,
    to_next,
    from_prev,
    from_next,
    pot,
    rho,
    up_out,
    up_in,
    down_out,
    down_in,
    own,
    part,
    side,
    raw_sem,
    in_sems,
    down_sems,
    up_sems,
    planes_down_sems,
    planes_up_sems,
    part_sems,
    out_sems,
):
    me = lax.axis_index("func")
    following = lax.rem(me + 1, count)
    preceding = lax.rem(me + count - 1, count)
    width = raw.shape[2]
    step = min(width, 256)

    def points(piece):
        return pl.ds(pl.multiple_of(piece * width, width), width)

    def raw_copy(piece):
        return pltpu.make_async_copy(
            boxes.at[:, points(piece)], raw.at[piece], raw_sem.at[piece]
        )

    small = [
        pltpu.make_async_copy(source, target, in_sems.at[place])
        for place, (source, target) in enumerate(
            (
                (sheets_in, sheets),
                (living_in, living),
                (weights_in, weights),
                (nucleus_in, nucleus),
                (applied_in, applied),
            )
        )
    ]
    for copy in small:
        copy.start()
    for piece in range(PIECES):
        raw_copy(piece).start()

    barrier = pltpu.get_barrier_semaphore()
    for neighbour in (preceding, following):
        pl.semaphore_signal(barrier, inc=1, device_id=(neighbour,), device_id_type=MESH)
    for copy in small:
        copy.wait()

    alive = jnp.broadcast_to(living[...], (SLOTS, count)).T
    lane = lax.broadcasted_iota(jnp.int32, (count, SLOTS), 1)
    owner = lax.broadcasted_iota(jnp.int32, (count, SLOTS), 0)
    starts[...] = jnp.where(lane < alive, sheets[...] - owner * DEPTH, 64).astype(F32)

    start = starts[pl.ds(me, 1), :]
    lanes = lax.broadcasted_iota(jnp.int32, (GROUPS, SLOTS), 1)
    rows = lax.broadcasted_iota(jnp.int32, (GROUPS, SLOTS), 0)
    spread = jnp.where(lanes // GROUP == rows, start, 0.0).astype(BF16)
    repeat = (
        lax.broadcasted_iota(jnp.int32, (SLOTS, SLOTS), 0) % GROUP
        == lax.broadcasted_iota(jnp.int32, (SLOTS, SLOTS), 1) // DEPTH
    )
    column_start = dot_nn(spread, jnp.where(repeat, 1.0, 0.0).astype(BF16))
    row = lax.broadcasted_iota(jnp.int32, (PLANES * GROUP, SLOTS), 0)
    column = lax.broadcasted_iota(jnp.int32, (PLANES * GROUP, SLOTS), 1)
    offset = jnp.where(
        row % GROUP == column // DEPTH, row // GROUP - column % DEPTH, -99
    ).astype(F32)
    for group in range(GROUPS):
        selector[group] = jnp.where(offset == column_start[group : group + 1, :], 1.0, 0.0).astype(BF16)
    wide_weights[...] = jnp.broadcast_to(weights[...], (SLOTS, SLOTS)).T

    def up_matrix(device):
        return rank_matrix(starts[pl.ds(device, 1), :])

    def down_matrix(device):
        first = starts[pl.ds(device, 1), :]
        return rank_matrix(jnp.where(first < 64.0, -first, first))

    up_order = up_matrix(me)
    down_order = down_matrix(me)
    order[0] = up_order.astype(BF16)
    order[1] = down_order.astype(BF16)
    back[0] = up_order.T.astype(BF16)
    back[1] = down_order.T.astype(BF16)

    def down_copy(piece):
        return pltpu.make_async_remote_copy(
            src_ref=down_out.at[piece],
            dst_ref=down_in.at[piece],
            send_sem=down_sems.at[0, piece],
            recv_sem=down_sems.at[1, piece],
            device_id=(following,),
            device_id_type=MESH,
        )

    def up_copy(piece):
        return pltpu.make_async_remote_copy(
            src_ref=up_out.at[piece],
            dst_ref=up_in.at[piece],
            send_sem=up_sems.at[0, piece],
            recv_sem=up_sems.at[1, piece],
            device_id=(preceding,),
            device_id_type=MESH,
        )

    def planes_down_copy(piece, length):
        return pltpu.make_async_remote_copy(
            src_ref=to_next.at[piece, pl.ds(0, length)],
            dst_ref=from_prev.at[piece, pl.ds(0, length)],
            send_sem=planes_down_sems.at[0, piece],
            recv_sem=planes_down_sems.at[1, piece],
            device_id=(following,),
            device_id_type=MESH,
        )

    def planes_up_copy(piece, length):
        return pltpu.make_async_remote_copy(
            src_ref=to_prev.at[piece, pl.ds(0, length)],
            dst_ref=from_next.at[piece, pl.ds(0, length)],
            send_sem=planes_up_sems.at[0, piece],
            recv_sem=planes_up_sems.at[1, piece],
            device_id=(preceding,),
            device_id_type=MESH,
        )

    def place(piece):
        raw_copy(piece).wait()
        for part_of in range(width // step):
            columns = pl.ds(part_of * step, step)
            columns_of_all = pl.ds(pl.multiple_of(piece * width + part_of * step, step), step)
            dens = jnp.zeros((PLANES, DEPTH, step), F32)
            for group in range(GROUPS):
                source = raw[piece, group * GROUP * DEPTH : (group + 1) * GROUP * DEPTH, columns]
                placed = dot_nn(selector[group], source).reshape(PLANES, GROUP, step)
                stack[piece, :, group * GROUP : (group + 1) * GROUP, columns] = placed.astype(BF16)
                weight = wide_weights[group * GROUP : (group + 1) * GROUP, :]
                weight = jnp.concatenate([weight] * (step // SLOTS), axis=1)
                terms = placed * placed * weight[None]
                dens += terms[:, :DEPTH] + terms[:, DEPTH:]
            dens = jnp.sum(dens, axis=1)
            down_out[piece, : DEPTH - 1, columns] = dens[DEPTH:]
            down_out[piece, DEPTH - 1 :, columns] = jnp.zeros((1, step), F32)
            up_out[piece, 0, :, columns] = nucleus[:, columns_of_all] + dens[:DEPTH]
            up_out[piece, 1, :, columns] = applied[:, columns_of_all]

    def pack_up(piece, level):
        rows = pl.ds(FIRST[level], ROOM[level])
        to_prev[piece, rows, :] = dot_nn(
            order[0, : ROOM[level], :], stack[piece, level, :SLOTS, :]
        ).astype(BF16)

    def pack_down(piece, level):
        rows = pl.ds(FIRST[level], ROOM[level])
        to_next[piece, rows, :] = dot_nn(
            order[1, : ROOM[level], :], stack[piece, 2 * DEPTH - 2 - level, :SLOTS, :]
        ).astype(BF16)

    def pack_and_send(piece):
        down_copy(piece).start()
        up_copy(piece).start()
        for level in range(LEVELS - 1):
            pack_up(piece, level)
            pack_down(piece, level)

        @pl.when(piece < PIECES // 2)
        def _():
            pack_up(piece, LEVELS - 1)
            planes_up_copy(piece, MANY).start()
            planes_down_copy(piece, FEW).start()

        @pl.when(piece >= PIECES // 2)
        def _():
            pack_down(piece, LEVELS - 1)
            planes_up_copy(piece, FEW).start()
            planes_down_copy(piece, MANY).start()

    place(0)
    pl.semaphore_wait(barrier, 2)
    pack_and_send(jnp.int32(0))

    def place_piece(piece, carry):
        place(piece)
        pack_and_send(piece)
        return carry

    lax.fori_loop(1, PIECES, place_piece, 0)

    over = jnp.zeros((count, 1), F32)
    first = starts[...]
    for level in range(LEVELS):
        low = jnp.sum(jnp.where(first <= level, 1.0, 0.0), axis=1, keepdims=True)
        high = jnp.sum(
            jnp.where((first >= DEPTH - 1 - level) & (first < 64.0), 1.0, 0.0), axis=1, keepdims=True
        )
        over = jnp.maximum(over, jnp.maximum(low, high) - ROOM[level])
    over_out[0] = jnp.max(over)

    own[...] = jnp.zeros_like(own)

    def own_piece(piece, carry):
        down_copy(piece).wait()
        up_copy(piece).wait()
        density = up_out[piece, 0] + down_in[piece]
        rho[:, points(piece)] = density
        pot[piece, :DEPTH] = up_out[piece, 1] - 0.9847 * cube_root(density)
        pot[piece, DEPTH:] = up_in[piece, 1] - 0.9847 * cube_root(up_in[piece, 0] + down_out[piece])
        total = own[...]
        for plane in range(PLANES):
            phi = stack[piece, plane, :SLOTS, :]
            stack[piece, plane, SLOTS:, :] = (phi.astype(F32) * pot[piece, plane : plane + 1, :]).astype(BF16)
            total += dot_nt(phi, stack[piece, plane])
        own[...] = total
        return carry

    lax.fori_loop(0, PIECES, own_piece, 0)
    rho_copy = pltpu.make_async_copy(rho, rho_out, out_sems.at[0])
    own_copy = pltpu.make_async_copy(own, own_out, out_sems.at[1])
    back_copy = pltpu.make_async_copy(back, back_out, out_sems.at[2])
    rho_copy.start()
    own_copy.start()
    back_copy.start()

    part[...] = jnp.zeros_like(part)

    def cross_next(piece, level):
        part[0, : ROOM[level], :] += dot_nt(
            from_next[piece, FIRST[level] : FIRST[level] + ROOM[level], :],
            stack[piece, DEPTH + level],
        )

    def cross_prev(piece, level):
        part[1, : ROOM[level], :] += dot_nt(
            from_prev[piece, FIRST[level] : FIRST[level] + ROOM[level], :],
            stack[piece, DEPTH - 2 - level],
        )

    def cross_piece(piece, carry):
        @pl.when(piece < PIECES // 2)
        def _():
            planes_up_copy(piece, MANY).wait()
            planes_down_copy(piece, FEW).wait()
            cross_next(piece, LEVELS - 1)

        @pl.when(piece >= PIECES // 2)
        def _():
            planes_up_copy(piece, FEW).wait()
            planes_down_copy(piece, MANY).wait()
            cross_prev(piece, LEVELS - 1)

        for level in range(LEVELS - 1):
            cross_next(piece, level)
            cross_prev(piece, level)
        return carry

    lax.fori_loop(0, PIECES, cross_piece, 0)

    def part_copy(which, target):
        return pltpu.make_async_remote_copy(
            src_ref=part.at[which, pl.ds(0, PARTS)],
            dst_ref=part_in.at[which],
            send_sem=part_sems.at[0, which],
            recv_sem=part_sems.at[1, which],
            device_id=(target,),
            device_id_type=MESH,
        )

    part_to_next = part_copy(0, following)
    part_to_prev = part_copy(1, preceding)
    part_to_next.start()
    part_to_prev.start()
    side[0] = select_columns(part[0].T, up_matrix(following).astype(BF16))
    side[1] = select_columns(part[1].T, down_matrix(preceding).astype(BF16))
    side_copy = pltpu.make_async_copy(side, side_out, out_sems.at[3])
    side_copy.start()
    rho_copy.wait()
    own_copy.wait()
    back_copy.wait()
    side_copy.wait()
    part_to_next.wait()
    part_to_prev.wait()


def finish_kernel(scale, rho, own, side, part_in, back, rho_out, ham_out, ovl_out):
    rho_out[...] = rho[...]
    none = jnp.zeros((SLOTS - PARTS, 2 * SLOTS), F32)
    from_prev = select_rows(back[0], jnp.concatenate([part_in[0], none], axis=0))
    from_next = select_rows(back[1], jnp.concatenate([part_in[1], none], axis=0))
    ovl_out[:, :SLOTS] = (side[1, :SLOTS, :] + from_prev[:, :SLOTS]) * scale
    ham_out[:, :SLOTS] = (side[1, SLOTS:, :] + from_prev[:, SLOTS:]) * scale
    ovl_out[:, SLOTS : 2 * SLOTS] = own[:, :SLOTS] * scale
    ham_out[:, SLOTS : 2 * SLOTS] = own[:, SLOTS:] * scale
    ovl_out[:, 2 * SLOTS :] = (side[0, :SLOTS, :] + from_next[:, :SLOTS]) * scale
    ham_out[:, 2 * SLOTS :] = (side[0, SLOTS:, :] + from_next[:, SLOTS:]) * scale


def full_kernel(
    count,
    boxes,
    weights,
    living,
    sheets,
    nucleus,
    applied,
    rho_out,
    ham_out,
    ovl_out,
    raw,
    selector,
    wide_weights,
    stack,
    from_prev,
    from_next,
    dens,
    pot,
    rho,
    up_out,
    up_in,
    down_out,
    down_in,
    own,
    part,
    part_in,
    ham,
    ovl,
    raw_sem,
    down_sems,
    up_sems,
    planes_down_sems,
    planes_up_sems,
    plane_sems,
    part_sems,
    out_sems,
):
    me = lax.axis_index("func")
    following = lax.rem(me + 1, count)
    preceding = lax.rem(me + count - 1, count)
    width = raw.shape[2]

    def points(piece):
        return pl.ds(pl.multiple_of(piece * width, width), width)

    def raw_copy(piece):
        return pltpu.make_async_copy(
            boxes.at[:, points(piece)], raw.at[piece], raw_sem.at[piece]
        )

    for piece in range(PIECES):
        raw_copy(piece).start()

    barrier = pltpu.get_barrier_semaphore()
    for neighbour in (preceding, following):
        pl.semaphore_signal(barrier, inc=1, device_id=(neighbour,), device_id_type=MESH)

    start = (sheets[pl.ds(me, 1), :] - me * DEPTH).astype(F32)
    lane = lax.broadcasted_iota(jnp.int32, (1, SLOTS), 1)
    start = jnp.where(lane < living[me], start, 64.0)
    lanes = lax.broadcasted_iota(jnp.int32, (GROUPS, SLOTS), 1)
    rows = lax.broadcasted_iota(jnp.int32, (GROUPS, SLOTS), 0)
    spread = jnp.where(lanes // GROUP == rows, start, 0.0).astype(BF16)
    repeat = (
        lax.broadcasted_iota(jnp.int32, (SLOTS, SLOTS), 0) % GROUP
        == lax.broadcasted_iota(jnp.int32, (SLOTS, SLOTS), 1) // DEPTH
    )
    column_start = jnp.dot(
        spread, jnp.where(repeat, 1.0, 0.0).astype(BF16), preferred_element_type=F32
    )
    row = lax.broadcasted_iota(jnp.int32, (PLANES * GROUP, SLOTS), 0)
    column = lax.broadcasted_iota(jnp.int32, (PLANES * GROUP, SLOTS), 1)
    offset = jnp.where(
        row % GROUP == column // DEPTH, row // GROUP - column % DEPTH, -99
    ).astype(F32)
    for group in range(GROUPS):
        selector[group] = jnp.where(offset == column_start[group : group + 1, :], 1.0, 0.0).astype(BF16)
    wide_weights[...] = jnp.broadcast_to(weights[...], (SLOTS, SLOTS)).T

    pl.semaphore_wait(barrier, 2)

    def down_copy(piece):
        return pltpu.make_async_remote_copy(
            src_ref=down_out.at[piece],
            dst_ref=down_in.at[piece],
            send_sem=down_sems.at[0, piece],
            recv_sem=down_sems.at[1, piece],
            device_id=(following,),
            device_id_type=MESH,
        )

    def up_copy(piece):
        return pltpu.make_async_remote_copy(
            src_ref=up_out.at[piece],
            dst_ref=up_in.at[piece],
            send_sem=up_sems.at[0, piece],
            recv_sem=up_sems.at[1, piece],
            device_id=(preceding,),
            device_id_type=MESH,
        )

    def planes_down_copy(piece):
        return pltpu.make_async_remote_copy(
            src_ref=stack.at[piece, pl.ds(DEPTH + 4, 3), pl.ds(0, SLOTS), :],
            dst_ref=from_prev.at[piece, pl.ds(1, 3)],
            send_sem=planes_down_sems.at[0, piece],
            recv_sem=planes_down_sems.at[1, piece],
            device_id=(following,),
            device_id_type=MESH,
        )

    def planes_up_copy(piece):
        return pltpu.make_async_remote_copy(
            src_ref=stack.at[piece, pl.ds(0, 3), pl.ds(0, SLOTS), :],
            dst_ref=from_next.at[piece, pl.ds(0, 3)],
            send_sem=planes_up_sems.at[0, piece],
            recv_sem=planes_up_sems.at[1, piece],
            device_id=(preceding,),
            device_id_type=MESH,
        )

    def plane_up_copy(piece):
        return pltpu.make_async_remote_copy(
            src_ref=stack.at[piece, 3, pl.ds(0, SLOTS), :],
            dst_ref=from_next.at[piece, 3],
            send_sem=plane_sems.at[0, piece],
            recv_sem=plane_sems.at[1, piece],
            device_id=(preceding,),
            device_id_type=MESH,
        )

    def plane_down_copy(piece):
        return pltpu.make_async_remote_copy(
            src_ref=stack.at[piece, DEPTH + 3, pl.ds(0, SLOTS), :],
            dst_ref=from_prev.at[piece, 0],
            send_sem=plane_sems.at[0, piece],
            recv_sem=plane_sems.at[1, piece],
            device_id=(following,),
            device_id_type=MESH,
        )

    def place_piece(piece, carry):
        raw_copy(piece).wait()
        dens[...] = jnp.zeros_like(dens)

        def place_group(group, carry):
            slots = pl.ds(pl.multiple_of(group * GROUP, GROUP), GROUP)
            source = raw[piece, pl.ds(pl.multiple_of(group * GROUP * DEPTH, GROUP * DEPTH), GROUP * DEPTH), :]
            placed = jnp.dot(selector[group], source, preferred_element_type=F32)
            placed = placed.reshape(PLANES, GROUP, width)
            stack[piece, :, slots, :] = placed.astype(BF16)
            weight = jnp.concatenate([wide_weights[slots, :]] * (width // SLOTS), axis=1)
            terms = placed * placed * weight[None]
            dens[...] += terms[:, :DEPTH] + terms[:, DEPTH:]
            return carry

        lax.fori_loop(0, GROUPS, place_group, 0)
        down_out[piece] = jnp.zeros_like(down_out[piece])
        down_out[piece, : DEPTH - 1] = jnp.sum(dens[DEPTH:], axis=1)
        up_out[piece, 0] = nucleus[:, points(piece)] + jnp.sum(dens[:DEPTH], axis=1)
        up_out[piece, 1] = applied[:, points(piece)]
        down_copy(piece).start()
        up_copy(piece).start()
        planes_down_copy(piece).start()
        planes_up_copy(piece).start()

        @pl.when(piece < PIECES // 2)
        def _():
            plane_up_copy(piece).start()

        @pl.when(piece >= PIECES // 2)
        def _():
            plane_down_copy(piece).start()

        return carry

    lax.fori_loop(0, PIECES, place_piece, 0)

    own[...] = jnp.zeros_like(own)

    def own_piece(piece, carry):
        down_copy(piece).wait()
        up_copy(piece).wait()
        density = up_out[piece, 0] + down_in[piece]
        rho[:, points(piece)] = density
        pot[piece, :DEPTH] = up_out[piece, 1] - 0.9847 * cube_root(density)
        pot[piece, DEPTH:] = up_in[piece, 1] - 0.9847 * cube_root(up_in[piece, 0] + down_out[piece])
        total = own[...]
        for plane in range(PLANES):
            phi = stack[piece, plane, :SLOTS, :]
            stack[piece, plane, SLOTS:, :] = (phi.astype(F32) * pot[piece, plane : plane + 1, :]).astype(BF16)
            total += dot_nt(phi, stack[piece, plane])
        own[...] = total
        return carry

    lax.fori_loop(0, PIECES, own_piece, 0)
    rho_copy = pltpu.make_async_copy(rho, rho_out, out_sems.at[0])
    rho_copy.start()

    scale = 1.0 / (DEPTH * width * PIECES)
    part[...] = jnp.zeros_like(part)

    def cross_piece(piece, carry):
        planes_up_copy(piece).wait()
        planes_down_copy(piece).wait()
        total = part[0]
        for shared in range(3):
            total += dot_nt(from_next[piece, shared], stack[piece, DEPTH + shared])
        part[0] = total
        total = part[1]
        for shared in range(4, 7):
            total += dot_nt(from_prev[piece, shared - 3], stack[piece, shared])
        part[1] = total

        @pl.when(piece < PIECES // 2)
        def _():
            plane_up_copy(piece).wait()
            part[0] += dot_nt(from_next[piece, 3], stack[piece, DEPTH + 3])

        @pl.when(piece >= PIECES // 2)
        def _():
            plane_down_copy(piece).wait()
            part[1] += dot_nt(from_prev[piece, 0], stack[piece, 3])

        return carry

    lax.fori_loop(0, PIECES, cross_piece, 0)

    def part_copy(side, target):
        return pltpu.make_async_remote_copy(
            src_ref=part.at[side],
            dst_ref=part_in.at[side],
            send_sem=part_sems.at[0, side],
            recv_sem=part_sems.at[1, side],
            device_id=(target,),
            device_id_type=MESH,
        )

    to_next = part_copy(0, following)
    to_prev = part_copy(1, preceding)
    to_next.start()
    to_prev.start()
    ovl[:, SLOTS : 2 * SLOTS] = own[:, :SLOTS] * scale
    ham[:, SLOTS : 2 * SLOTS] = own[:, SLOTS:] * scale
    ovl_next = part[0, :, :SLOTS].T
    ham_next = part[0, :, SLOTS:].T
    ovl_prev = part[1, :, :SLOTS].T
    ham_prev = part[1, :, SLOTS:].T
    to_next.wait()
    to_prev.wait()
    ovl[:, :SLOTS] = (ovl_prev + part_in[0, :, :SLOTS]) * scale
    ham[:, :SLOTS] = (ham_prev + part_in[0, :, SLOTS:]) * scale
    ovl[:, 2 * SLOTS :] = (ovl_next + part_in[1, :, :SLOTS]) * scale
    ham[:, 2 * SLOTS :] = (ham_next + part_in[1, :, SLOTS:]) * scale
    ovl_copy = pltpu.make_async_copy(ovl, ovl_out, out_sems.at[1])
    ham_copy = pltpu.make_async_copy(ham, ham_out, out_sems.at[2])
    ovl_copy.start()
    ham_copy.start()
    rho_copy.wait()
    ovl_copy.wait()
    ham_copy.wait()


def full_call(
    basis_wavefunctions,
    filling_weights,
    living_per_unit,
    starting_sheets,
    nucleus_charge,
    applied_field,
):
    slots, depth, points = basis_wavefunctions.shape
    count = lax.axis_size("func")
    width = points // PIECES
    vmem = pl.BlockSpec(memory_space=pltpu.VMEM)
    anywhere = pl.BlockSpec(memory_space=pl.ANY)
    pair = pltpu.SemaphoreType.DMA((2, PIECES))
    return pl.pallas_call(
        functools.partial(full_kernel, count),
        out_shape=(
            jax.ShapeDtypeStruct((depth, points), F32),
            jax.ShapeDtypeStruct((slots, 3 * slots), F32),
            jax.ShapeDtypeStruct((slots, 3 * slots), F32),
        ),
        in_specs=[
            anywhere,
            vmem,
            pl.BlockSpec(memory_space=pltpu.SMEM),
            vmem,
            vmem,
            vmem,
        ],
        out_specs=(anywhere, anywhere, anywhere),
        scratch_shapes=[
            pltpu.VMEM((PIECES, slots * depth, width), BF16),
            pltpu.VMEM((GROUPS, PLANES * GROUP, slots), BF16),
            pltpu.VMEM((slots, slots), F32),
            pltpu.VMEM((PIECES, PLANES, 2 * slots, width), BF16),
            pltpu.VMEM((PIECES, 4, slots, width), BF16),
            pltpu.VMEM((PIECES, 4, slots, width), BF16),
            pltpu.VMEM((PLANES, DEPTH, width), F32),
            pltpu.VMEM((PIECES, 2 * DEPTH, width), F32),
            pltpu.VMEM((depth, points), F32),
            pltpu.VMEM((PIECES, 2, DEPTH, width), F32),
            pltpu.VMEM((PIECES, 2, DEPTH, width), F32),
            pltpu.VMEM((PIECES, DEPTH, width), F32),
            pltpu.VMEM((PIECES, DEPTH, width), F32),
            pltpu.VMEM((slots, 2 * slots), F32),
            pltpu.VMEM((2, slots, 2 * slots), F32),
            pltpu.VMEM((2, slots, 2 * slots), F32),
            pltpu.VMEM((slots, 3 * slots), F32),
            pltpu.VMEM((slots, 3 * slots), F32),
            pltpu.SemaphoreType.DMA((PIECES,)),
            pair,
            pair,
            pair,
            pair,
            pair,
            pltpu.SemaphoreType.DMA((2, 2)),
            pltpu.SemaphoreType.DMA((3,)),
        ],
        compiler_params=pltpu.CompilerParams(
            collective_id=1, has_side_effects=True, vmem_limit_bytes=56 * 2**20
        ),
        cost_estimate=pl.CostEstimate(
            flops=4 * 10**9, bytes_accessed=5 * 2**20, transcendentals=2**16
        ),
    )(
        basis_wavefunctions.reshape(slots * depth, points),
        filling_weights.reshape(1, slots),
        living_per_unit,
        starting_sheets.reshape(count, slots),
        nucleus_charge,
        applied_field,
    )


def per_device(
    basis_wavefunctions,
    filling_weights,
    living_per_unit,
    starting_sheets,
    nucleus_charge,
    applied_field,
):
    slots, depth, points = basis_wavefunctions.shape
    count = lax.axis_size("func")
    width = points // PIECES
    anywhere = pl.BlockSpec(memory_space=pl.ANY)
    pair = pltpu.SemaphoreType.DMA((2, PIECES))
    rho, own, side, part_in, back, over = pl.pallas_call(
        functools.partial(packed_kernel, count),
        out_shape=(
            jax.ShapeDtypeStruct((depth, points), F32),
            jax.ShapeDtypeStruct((slots, 2 * slots), F32),
            jax.ShapeDtypeStruct((2, 2 * slots, slots), F32),
            jax.ShapeDtypeStruct((2, PARTS, 2 * slots), F32),
            jax.ShapeDtypeStruct((2, slots, slots), BF16),
            jax.ShapeDtypeStruct((1,), F32),
        ),
        in_specs=[anywhere] * 6,
        out_specs=(anywhere,) * 5 + (pl.BlockSpec(memory_space=pltpu.SMEM),),
        scratch_shapes=[
            pltpu.VMEM((PIECES, slots * depth, width), BF16),
            pltpu.VMEM((1, slots), F32),
            pltpu.VMEM((1, count), jnp.int32),
            pltpu.VMEM((count, slots), jnp.int32),
            pltpu.VMEM((depth, points), F32),
            pltpu.VMEM((depth, points), F32),
            pltpu.VMEM((count, slots), F32),
            pltpu.VMEM((GROUPS, PLANES * GROUP, slots), BF16),
            pltpu.VMEM((slots, slots), F32),
            pltpu.VMEM((2, slots, slots), BF16),
            pltpu.VMEM((2, slots, slots), BF16),
            pltpu.VMEM((PIECES, PLANES, 2 * slots, width), BF16),
            pltpu.VMEM((PIECES, MANY, width), BF16),
            pltpu.VMEM((PIECES, MANY, width), BF16),
            pltpu.VMEM((PIECES, MANY, width), BF16),
            pltpu.VMEM((PIECES, MANY, width), BF16),
            pltpu.VMEM((PIECES, 2 * DEPTH, width), F32),
            pltpu.VMEM((depth, points), F32),
            pltpu.VMEM((PIECES, 2, DEPTH, width), F32),
            pltpu.VMEM((PIECES, 2, DEPTH, width), F32),
            pltpu.VMEM((PIECES, DEPTH, width), F32),
            pltpu.VMEM((PIECES, DEPTH, width), F32),
            pltpu.VMEM((slots, 2 * slots), F32),
            pltpu.VMEM((2, slots, 2 * slots), F32),
            pltpu.VMEM((2, 2 * slots, slots), F32),
            pltpu.SemaphoreType.DMA((PIECES,)),
            pltpu.SemaphoreType.DMA((5,)),
            pair,
            pair,
            pair,
            pair,
            pltpu.SemaphoreType.DMA((2, 2)),
            pltpu.SemaphoreType.DMA((4,)),
        ],
        compiler_params=pltpu.CompilerParams(
            collective_id=0, has_side_effects=True, vmem_limit_bytes=56 * 2**20
        ),
        cost_estimate=pl.CostEstimate(
            flops=4 * 10**9, bytes_accessed=5 * 2**20, transcendentals=2**16
        ),
    )(
        basis_wavefunctions.reshape(slots * depth, points),
        filling_weights.reshape(1, slots),
        living_per_unit.reshape(1, count),
        starting_sheets.reshape(count, slots),
        nucleus_charge,
        applied_field,
    )

    def finish():
        return tuple(
            pl.pallas_call(
                functools.partial(finish_kernel, 1.0 / (depth * points)),
                out_shape=(
                    jax.ShapeDtypeStruct((depth, points), F32),
                    jax.ShapeDtypeStruct((slots, 3 * slots), F32),
                    jax.ShapeDtypeStruct((slots, 3 * slots), F32),
                ),
            )(rho, own, side, part_in, back)
        )

    def in_full():
        return tuple(
            full_call(
                basis_wavefunctions,
                filling_weights,
                living_per_unit,
                starting_sheets,
                nucleus_charge,
                applied_field,
            )
        )

    return lax.cond(over[0] > 0.0, in_full, finish)


def solution(mesh):
    return jax.shard_map(
        per_device,
        mesh=mesh,
        in_specs=(P("func", None, None), P("func"), P(), P(), P("func", None), P("func", None)),
        out_specs=(P("func", None), P("func", None), P("func", None)),
        check_vma=False,
    )
```

```python
import functools

import jax
import jax.numpy as jnp
from jax import lax
from jax.experimental import pallas as pl
from jax.experimental.pallas import tpu as pltpu
from jax.sharding import PartitionSpec as P

MESH = pl.DeviceIdType.MESH
F32 = jnp.float32
BF16 = jnp.bfloat16

SLOTS = 128
DEPTH = 8
PLANES = 2 * DEPTH - 1
GROUP = 16
GROUPS = SLOTS // GROUP
PIECES = 4
LEVELS = 4
ROOM = (32, 64, 80, 96)
FIRST = (0, 32, 96, 176)
FEW, MANY = 176, 272
PARTS = 96
LAYERS = 4
UP_PIECES = 1


def dot_nt(a, b):
    return lax.dot_general(a, b, (((1,), (1,)), ((), ())), preferred_element_type=F32)


def cube_root(x):
    y = jnp.exp(jnp.log(x) * (1.0 / 3.0))
    return (2.0 * y + x / (y * y)) * (1.0 / 3.0)


def dot_nn(a, b):
    return lax.dot_general(a, b, (((1,), (0,)), ((), ())), preferred_element_type=F32)


def select_rows(one_hot, values):
    high = values.astype(BF16)
    low = (values - high.astype(F32)).astype(BF16)
    return dot_nn(one_hot, high) + dot_nn(one_hot, low)


def select_columns(values, one_hot):
    high = values.astype(BF16)
    low = (values - high.astype(F32)).astype(BF16)
    return dot_nn(high, one_hot) + dot_nn(low, one_hot)


def rank_matrix(key):
    row = lax.broadcasted_iota(jnp.int32, (SLOTS, SLOTS), 0)
    column = lax.broadcasted_iota(jnp.int32, (SLOTS, SLOTS), 1)
    wide = jnp.broadcast_to(key, (SLOTS, SLOTS))
    tall = wide.T
    before = jnp.where((tall < wide) | ((tall == wide) & (row < column)), 1.0, 0.0)
    rank = jnp.sum(before, axis=0, keepdims=True)
    return jnp.where(row.astype(F32) == rank, 1.0, 0.0)


def packed_kernel(
    count,
    boxes,
    weights_in,
    living_in,
    sheets_in,
    nucleus_in,
    applied_in,
    rho_out,
    own_out,
    side_out,
    part_in,
    back_out,
    over_out,
    raw,
    weights,
    living,
    sheets,
    nucleus,
    applied,
    starts,
    selector,
    wide_weights,
    order,
    back,
    stack,
    to_prev,
    to_next,
    from_prev,
    from_next,
    pot,
    rho,
    base,
    up_out,
    up_in,
    down_out,
    down_in,
    own,
    part,
    side,
    raw_sem,
    in_sems,
    down_sems,
    up_sems,
    planes_down_sems,
    planes_up_sems,
    part_sems,
    out_sems,
):
    me = lax.axis_index("func")
    following = lax.rem(me + 1, count)
    preceding = lax.rem(me + count - 1, count)
    width = raw.shape[2]
    step = min(width, 256)

    def points(piece):
        return pl.ds(pl.multiple_of(piece * width, width), width)

    def raw_copy(piece):
        return pltpu.make_async_copy(
            boxes.at[:, points(piece)], raw.at[piece], raw_sem.at[piece]
        )

    small = [
        pltpu.make_async_copy(source, target, in_sems.at[place])
        for place, (source, target) in enumerate(
            (
                (sheets_in, sheets),
                (living_in, living),
                (weights_in, weights),
                (nucleus_in, nucleus),
                (applied_in, applied),
            )
        )
    ]
    for copy in small:
        copy.start()
    for piece in range(PIECES):
        raw_copy(piece).start()

    barrier = pltpu.get_barrier_semaphore()
    for neighbour in (preceding, following):
        pl.semaphore_signal(barrier, inc=1, device_id=(neighbour,), device_id_type=MESH)
    for copy in small:
        copy.wait()

    alive = jnp.broadcast_to(living[...], (SLOTS, count)).T
    lane = lax.broadcasted_iota(jnp.int32, (count, SLOTS), 1)
    owner = lax.broadcasted_iota(jnp.int32, (count, SLOTS), 0)
    starts[...] = jnp.where(lane < alive, sheets[...] - owner * DEPTH, 64).astype(F32)

    start = starts[pl.ds(me, 1), :]
    lanes = lax.broadcasted_iota(jnp.int32, (GROUPS, SLOTS), 1)
    rows = lax.broadcasted_iota(jnp.int32, (GROUPS, SLOTS), 0)
    spread = jnp.where(lanes // GROUP == rows, start, 0.0).astype(BF16)
    repeat = (
        lax.broadcasted_iota(jnp.int32, (SLOTS, SLOTS), 0) % GROUP
        == lax.broadcasted_iota(jnp.int32, (SLOTS, SLOTS), 1) // DEPTH
    )
    column_start = dot_nn(spread, jnp.where(repeat, 1.0, 0.0).astype(BF16))
    row = lax.broadcasted_iota(jnp.int32, (PLANES * GROUP, SLOTS), 0)
    column = lax.broadcasted_iota(jnp.int32, (PLANES * GROUP, SLOTS), 1)
    offset = jnp.where(
        row % GROUP == column // DEPTH, row // GROUP - column % DEPTH, -99
    ).astype(F32)
    for group in range(GROUPS):
        selector[group] = jnp.where(offset == column_start[group : group + 1, :], 1.0, 0.0).astype(BF16)
    wide_weights[...] = jnp.broadcast_to(weights[...], (SLOTS, SLOTS)).T

    def up_matrix(device):
        return rank_matrix(starts[pl.ds(device, 1), :])

    def down_matrix(device):
        first = starts[pl.ds(device, 1), :]
        return rank_matrix(jnp.where(first < 64.0, -first, first))

    up_order = up_matrix(me)
    down_order = down_matrix(me)
    order[0] = up_order.astype(BF16)
    order[1] = down_order.astype(BF16)
    back[0] = up_order.T.astype(BF16)
    back[1] = down_order.T.astype(BF16)

    def down_copy(piece):
        return pltpu.make_async_remote_copy(
            src_ref=down_out.at[piece],
            dst_ref=down_in.at[piece],
            send_sem=down_sems.at[0, piece],
            recv_sem=down_sems.at[1, piece],
            device_id=(following,),
            device_id_type=MESH,
        )

    def up_copy(piece):
        return pltpu.make_async_remote_copy(
            src_ref=up_out.at[piece],
            dst_ref=up_in.at[piece],
            send_sem=up_sems.at[0, piece],
            recv_sem=up_sems.at[1, piece],
            device_id=(preceding,),
            device_id_type=MESH,
        )

    def planes_down_copy(piece, length):
        return pltpu.make_async_remote_copy(
            src_ref=to_next.at[piece, pl.ds(0, length)],
            dst_ref=from_prev.at[piece, pl.ds(0, length)],
            send_sem=planes_down_sems.at[0, piece],
            recv_sem=planes_down_sems.at[1, piece],
            device_id=(following,),
            device_id_type=MESH,
        )

    def planes_up_copy(piece, length):
        return pltpu.make_async_remote_copy(
            src_ref=to_prev.at[piece, pl.ds(0, length)],
            dst_ref=from_next.at[piece, pl.ds(0, length)],
            send_sem=planes_up_sems.at[0, piece],
            recv_sem=planes_up_sems.at[1, piece],
            device_id=(preceding,),
            device_id_type=MESH,
        )

    def place(piece):
        raw_copy(piece).wait()
        for part_of in range(width // step):
            columns = pl.ds(part_of * step, step)
            columns_of_all = pl.ds(pl.multiple_of(piece * width + part_of * step, step), step)
            dens = jnp.zeros((PLANES, DEPTH, step), F32)
            for group in range(GROUPS):
                source = raw[piece, group * GROUP * DEPTH : (group + 1) * GROUP * DEPTH, columns]
                placed = dot_nn(selector[group], source).reshape(PLANES, GROUP, step)
                stack[piece, :, group * GROUP : (group + 1) * GROUP, columns] = placed.astype(BF16)
                weight = wide_weights[group * GROUP : (group + 1) * GROUP, :]
                weight = jnp.concatenate([weight] * (step // SLOTS), axis=1)
                terms = placed * placed * weight[None]
                dens += terms[:, :DEPTH] + terms[:, DEPTH:]
            dens = jnp.sum(dens, axis=1)
            down_out[piece, : DEPTH - 1, columns] = dens[DEPTH:]
            down_out[piece, DEPTH - 1 :, columns] = jnp.zeros((1, step), F32)
            below = nucleus[:, columns_of_all] + dens[:DEPTH]
            base[piece, :, columns] = below
            up_out[piece, :DEPTH, columns] = below.astype(BF16)
            up_out[piece, DEPTH:, columns] = applied[:, columns_of_all].astype(BF16)

    def pack_up(piece, level):
        rows = pl.ds(FIRST[level], ROOM[level])
        to_prev[piece, rows, :] = dot_nn(
            order[0, : ROOM[level], :], stack[piece, level, :SLOTS, :]
        ).astype(BF16)

    def pack_down(piece, level):
        rows = pl.ds(FIRST[level], ROOM[level])
        to_next[piece, rows, :] = dot_nn(
            order[1, : ROOM[level], :], stack[piece, 2 * DEPTH - 2 - level, :SLOTS, :]
        ).astype(BF16)

    def pack(piece):
        for level in range(LEVELS - 1):
            pack_up(piece, level)
            pack_down(piece, level)

        @pl.when(piece < UP_PIECES)
        def _():
            pack_up(piece, LEVELS - 1)

        @pl.when(piece >= UP_PIECES)
        def _():
            pack_down(piece, LEVELS - 1)

    def send_density(piece):
        down_copy(piece).start()
        up_copy(piece).start()

    def send_planes(piece):
        @pl.when(piece < UP_PIECES)
        def _():
            planes_up_copy(piece, MANY).start()
            planes_down_copy(piece, FEW).start()

        @pl.when(piece >= UP_PIECES)
        def _():
            planes_up_copy(piece, FEW).start()
            planes_down_copy(piece, MANY).start()

    def place_and_pack(piece, carry):
        place(piece)
        pack(piece)
        return carry

    late = lax.rem(me, max(count // LAYERS, 1)) == 0
    place_and_pack(jnp.int32(0), 0)

    @pl.when(late)
    def _():
        lax.fori_loop(1, PIECES, place_and_pack, 0)

    pl.semaphore_wait(barrier, 2)
    send_density(jnp.int32(0))

    @pl.when(late)
    def _():
        for piece in range(1, PIECES):
            send_density(piece)

    send_planes(jnp.int32(0))

    def next_piece(piece, carry):
        @pl.when(jnp.logical_not(late))
        def _():
            place(piece)
            send_density(piece)
            pack(piece)

        send_planes(piece)
        return carry

    lax.fori_loop(1, PIECES, next_piece, 0)

    over = jnp.zeros((count, 1), F32)
    first = starts[...]
    for level in range(LEVELS):
        low = jnp.sum(jnp.where(first <= level, 1.0, 0.0), axis=1, keepdims=True)
        high = jnp.sum(
            jnp.where((first >= DEPTH - 1 - level) & (first < 64.0), 1.0, 0.0), axis=1, keepdims=True
        )
        over = jnp.maximum(over, jnp.maximum(low, high) - ROOM[level])
    over_out[0] = jnp.max(over)

    own[...] = jnp.zeros_like(own)

    def own_piece(piece, carry):
        down_copy(piece).wait()
        up_copy(piece).wait()
        density = base[piece] + down_in[piece]
        rho[:, points(piece)] = density
        pot[piece, :DEPTH] = applied[:, points(piece)] - 0.9847 * cube_root(density)
        above = up_in[piece].astype(F32)
        pot[piece, DEPTH:] = above[DEPTH:] - 0.9847 * cube_root(above[:DEPTH] + down_out[piece])
        total = own[...]
        for plane in range(PLANES):
            phi = stack[piece, plane, :SLOTS, :]
            stack[piece, plane, SLOTS:, :] = (phi.astype(F32) * pot[piece, plane : plane + 1, :]).astype(BF16)
            total += dot_nt(phi, stack[piece, plane])
        own[...] = total
        return carry

    lax.fori_loop(0, PIECES, own_piece, 0)
    rho_copy = pltpu.make_async_copy(rho, rho_out, out_sems.at[0])
    own_copy = pltpu.make_async_copy(own, own_out, out_sems.at[1])
    back_copy = pltpu.make_async_copy(back, back_out, out_sems.at[2])
    rho_copy.start()
    own_copy.start()
    back_copy.start()

    part[...] = jnp.zeros_like(part)

    def cross_next(piece, level):
        part[0, : ROOM[level], :] += dot_nt(
            from_next[piece, FIRST[level] : FIRST[level] + ROOM[level], :],
            stack[piece, DEPTH + level],
        )

    def cross_prev(piece, level):
        part[1, : ROOM[level], :] += dot_nt(
            from_prev[piece, FIRST[level] : FIRST[level] + ROOM[level], :],
            stack[piece, DEPTH - 2 - level],
        )

    def cross_piece(piece, carry):
        @pl.when(piece < UP_PIECES)
        def _():
            planes_up_copy(piece, MANY).wait()
            planes_down_copy(piece, FEW).wait()
            cross_next(piece, LEVELS - 1)

        @pl.when(piece >= UP_PIECES)
        def _():
            planes_up_copy(piece, FEW).wait()
            planes_down_copy(piece, MANY).wait()
            cross_prev(piece, LEVELS - 1)

        for level in range(LEVELS - 1):
            cross_next(piece, level)
            cross_prev(piece, level)
        return carry

    lax.fori_loop(0, PIECES, cross_piece, 0)

    def part_copy(which, target):
        return pltpu.make_async_remote_copy(
            src_ref=part.at[which, pl.ds(0, PARTS)],
            dst_ref=part_in.at[which],
            send_sem=part_sems.at[0, which],
            recv_sem=part_sems.at[1, which],
            device_id=(target,),
            device_id_type=MESH,
        )

    part_to_next = part_copy(0, following)
    part_to_prev = part_copy(1, preceding)
    part_to_next.start()
    part_to_prev.start()
    side[0] = select_columns(part[0].T, up_matrix(following).astype(BF16))
    side[1] = select_columns(part[1].T, down_matrix(preceding).astype(BF16))
    side_copy = pltpu.make_async_copy(side, side_out, out_sems.at[3])
    side_copy.start()
    rho_copy.wait()
    own_copy.wait()
    back_copy.wait()
    side_copy.wait()
    part_to_next.wait()
    part_to_prev.wait()


def finish_kernel(scale, rho, own, side, part_in, back, rho_out, ham_out, ovl_out):
    rho_out[...] = rho[...]
    none = jnp.zeros((SLOTS - PARTS, 2 * SLOTS), F32)
    from_prev = select_rows(back[0], jnp.concatenate([part_in[0], none], axis=0))
    from_next = select_rows(back[1], jnp.concatenate([part_in[1], none], axis=0))
    ovl_out[:, :SLOTS] = (side[1, :SLOTS, :] + from_prev[:, :SLOTS]) * scale
    ham_out[:, :SLOTS] = (side[1, SLOTS:, :] + from_prev[:, SLOTS:]) * scale
    ovl_out[:, SLOTS : 2 * SLOTS] = own[:, :SLOTS] * scale
    ham_out[:, SLOTS : 2 * SLOTS] = own[:, SLOTS:] * scale
    ovl_out[:, 2 * SLOTS :] = (side[0, :SLOTS, :] + from_next[:, :SLOTS]) * scale
    ham_out[:, 2 * SLOTS :] = (side[0, SLOTS:, :] + from_next[:, SLOTS:]) * scale


def full_kernel(
    count,
    boxes,
    weights,
    living,
    sheets,
    nucleus,
    applied,
    side_out,
    raw,
    selector,
    wide_weights,
    stack,
    from_prev,
    from_next,
    dens,
    pot,
    up_out,
    up_in,
    down_out,
    down_in,
    part,
    part_in,
    side,
    raw_sem,
    down_sems,
    up_sems,
    planes_down_sems,
    planes_up_sems,
    plane_sems,
    part_sems,
    out_sem,
):
    me = lax.axis_index("func")
    following = lax.rem(me + 1, count)
    preceding = lax.rem(me + count - 1, count)
    width = raw.shape[2]

    def points(piece):
        return pl.ds(pl.multiple_of(piece * width, width), width)

    def raw_copy(piece):
        return pltpu.make_async_copy(
            boxes.at[:, points(piece)], raw.at[piece], raw_sem.at[piece]
        )

    for piece in range(PIECES):
        raw_copy(piece).start()

    barrier = pltpu.get_barrier_semaphore()
    for neighbour in (preceding, following):
        pl.semaphore_signal(barrier, inc=1, device_id=(neighbour,), device_id_type=MESH)

    start = (sheets[pl.ds(me, 1), :] - me * DEPTH).astype(F32)
    lane = lax.broadcasted_iota(jnp.int32, (1, SLOTS), 1)
    start = jnp.where(lane < living[me], start, 64.0)
    lanes = lax.broadcasted_iota(jnp.int32, (GROUPS, SLOTS), 1)
    rows = lax.broadcasted_iota(jnp.int32, (GROUPS, SLOTS), 0)
    spread = jnp.where(lanes // GROUP == rows, start, 0.0).astype(BF16)
    repeat = (
        lax.broadcasted_iota(jnp.int32, (SLOTS, SLOTS), 0) % GROUP
        == lax.broadcasted_iota(jnp.int32, (SLOTS, SLOTS), 1) // DEPTH
    )
    column_start = jnp.dot(
        spread, jnp.where(repeat, 1.0, 0.0).astype(BF16), preferred_element_type=F32
    )
    row = lax.broadcasted_iota(jnp.int32, (PLANES * GROUP, SLOTS), 0)
    column = lax.broadcasted_iota(jnp.int32, (PLANES * GROUP, SLOTS), 1)
    offset = jnp.where(
        row % GROUP == column // DEPTH, row // GROUP - column % DEPTH, -99
    ).astype(F32)
    for group in range(GROUPS):
        selector[group] = jnp.where(offset == column_start[group : group + 1, :], 1.0, 0.0).astype(BF16)
    wide_weights[...] = jnp.broadcast_to(weights[...], (SLOTS, SLOTS)).T

    pl.semaphore_wait(barrier, 2)

    def down_copy(piece):
        return pltpu.make_async_remote_copy(
            src_ref=down_out.at[piece],
            dst_ref=down_in.at[piece],
            send_sem=down_sems.at[0, piece],
            recv_sem=down_sems.at[1, piece],
            device_id=(following,),
            device_id_type=MESH,
        )

    def up_copy(piece):
        return pltpu.make_async_remote_copy(
            src_ref=up_out.at[piece],
            dst_ref=up_in.at[piece],
            send_sem=up_sems.at[0, piece],
            recv_sem=up_sems.at[1, piece],
            device_id=(preceding,),
            device_id_type=MESH,
        )

    def planes_down_copy(piece):
        return pltpu.make_async_remote_copy(
            src_ref=stack.at[piece, pl.ds(DEPTH + 4, 3), pl.ds(0, SLOTS), :],
            dst_ref=from_prev.at[piece, pl.ds(1, 3)],
            send_sem=planes_down_sems.at[0, piece],
            recv_sem=planes_down_sems.at[1, piece],
            device_id=(following,),
            device_id_type=MESH,
        )

    def planes_up_copy(piece):
        return pltpu.make_async_remote_copy(
            src_ref=stack.at[piece, pl.ds(0, 3), pl.ds(0, SLOTS), :],
            dst_ref=from_next.at[piece, pl.ds(0, 3)],
            send_sem=planes_up_sems.at[0, piece],
            recv_sem=planes_up_sems.at[1, piece],
            device_id=(preceding,),
            device_id_type=MESH,
        )

    def plane_up_copy(piece):
        return pltpu.make_async_remote_copy(
            src_ref=stack.at[piece, 3, pl.ds(0, SLOTS), :],
            dst_ref=from_next.at[piece, 3],
            send_sem=plane_sems.at[0, piece],
            recv_sem=plane_sems.at[1, piece],
            device_id=(preceding,),
            device_id_type=MESH,
        )

    def plane_down_copy(piece):
        return pltpu.make_async_remote_copy(
            src_ref=stack.at[piece, DEPTH + 3, pl.ds(0, SLOTS), :],
            dst_ref=from_prev.at[piece, 0],
            send_sem=plane_sems.at[0, piece],
            recv_sem=plane_sems.at[1, piece],
            device_id=(following,),
            device_id_type=MESH,
        )

    def place_piece(piece, carry):
        raw_copy(piece).wait()
        dens[...] = jnp.zeros_like(dens)

        def place_group(group, carry):
            slots = pl.ds(pl.multiple_of(group * GROUP, GROUP), GROUP)
            source = raw[piece, pl.ds(pl.multiple_of(group * GROUP * DEPTH, GROUP * DEPTH), GROUP * DEPTH), :]
            placed = jnp.dot(selector[group], source, preferred_element_type=F32)
            placed = placed.reshape(PLANES, GROUP, width)
            stack[piece, :, slots, :] = placed.astype(BF16)
            weight = jnp.concatenate([wide_weights[slots, :]] * (width // SLOTS), axis=1)
            terms = placed * placed * weight[None]
            dens[...] += terms[:, :DEPTH] + terms[:, DEPTH:]
            return carry

        lax.fori_loop(0, GROUPS, place_group, 0)
        down_out[piece] = jnp.zeros_like(down_out[piece])
        down_out[piece, : DEPTH - 1] = jnp.sum(dens[DEPTH:], axis=1)
        up_out[piece, 0] = nucleus[:, points(piece)] + jnp.sum(dens[:DEPTH], axis=1)
        up_out[piece, 1] = applied[:, points(piece)]
        down_copy(piece).start()
        up_copy(piece).start()
        planes_down_copy(piece).start()
        planes_up_copy(piece).start()

        @pl.when(piece < PIECES // 2)
        def _():
            plane_up_copy(piece).start()

        @pl.when(piece >= PIECES // 2)
        def _():
            plane_down_copy(piece).start()

        return carry

    lax.fori_loop(0, PIECES, place_piece, 0)

    def own_piece(piece, carry):
        down_copy(piece).wait()
        up_copy(piece).wait()
        density = up_out[piece, 0] + down_in[piece]
        pot[piece, :DEPTH] = up_out[piece, 1] - 0.9847 * cube_root(density)
        pot[piece, DEPTH:] = up_in[piece, 1] - 0.9847 * cube_root(up_in[piece, 0] + down_out[piece])
        for plane in range(PLANES):
            phi = stack[piece, plane, :SLOTS, :]
            stack[piece, plane, SLOTS:, :] = (phi.astype(F32) * pot[piece, plane : plane + 1, :]).astype(BF16)
        return carry

    lax.fori_loop(0, PIECES, own_piece, 0)
    part[...] = jnp.zeros_like(part)

    def cross_piece(piece, carry):
        planes_up_copy(piece).wait()
        planes_down_copy(piece).wait()
        total = part[0]
        for shared in range(3):
            total += dot_nt(from_next[piece, shared], stack[piece, DEPTH + shared])
        part[0] = total
        total = part[1]
        for shared in range(4, 7):
            total += dot_nt(from_prev[piece, shared - 3], stack[piece, shared])
        part[1] = total

        @pl.when(piece < PIECES // 2)
        def _():
            plane_up_copy(piece).wait()
            part[0] += dot_nt(from_next[piece, 3], stack[piece, DEPTH + 3])

        @pl.when(piece >= PIECES // 2)
        def _():
            plane_down_copy(piece).wait()
            part[1] += dot_nt(from_prev[piece, 0], stack[piece, 3])

        return carry

    lax.fori_loop(0, PIECES, cross_piece, 0)

    def part_copy(side, target):
        return pltpu.make_async_remote_copy(
            src_ref=part.at[side],
            dst_ref=part_in.at[side],
            send_sem=part_sems.at[0, side],
            recv_sem=part_sems.at[1, side],
            device_id=(target,),
            device_id_type=MESH,
        )

    to_next = part_copy(0, following)
    to_prev = part_copy(1, preceding)
    to_next.start()
    to_prev.start()
    to_next.wait()
    to_prev.wait()
    side[0, :SLOTS] = part[0, :, :SLOTS].T + part_in[1, :, :SLOTS]
    side[0, SLOTS:] = part[0, :, SLOTS:].T + part_in[1, :, SLOTS:]
    side[1, :SLOTS] = part[1, :, :SLOTS].T + part_in[0, :, :SLOTS]
    side[1, SLOTS:] = part[1, :, SLOTS:].T + part_in[0, :, SLOTS:]
    side_copy = pltpu.make_async_copy(side, side_out, out_sem)
    side_copy.start()
    side_copy.wait()


def full_call(
    basis_wavefunctions,
    filling_weights,
    living_per_unit,
    starting_sheets,
    nucleus_charge,
    applied_field,
):
    slots, depth, points = basis_wavefunctions.shape
    count = lax.axis_size("func")
    width = points // PIECES
    vmem = pl.BlockSpec(memory_space=pltpu.VMEM)
    anywhere = pl.BlockSpec(memory_space=pl.ANY)
    pair = pltpu.SemaphoreType.DMA((2, PIECES))
    return pl.pallas_call(
        functools.partial(full_kernel, count),
        out_shape=jax.ShapeDtypeStruct((2, 2 * slots, slots), F32),
        in_specs=[
            anywhere,
            vmem,
            pl.BlockSpec(memory_space=pltpu.SMEM),
            vmem,
            vmem,
            vmem,
        ],
        out_specs=anywhere,
        scratch_shapes=[
            pltpu.VMEM((PIECES, slots * depth, width), BF16),
            pltpu.VMEM((GROUPS, PLANES * GROUP, slots), BF16),
            pltpu.VMEM((slots, slots), F32),
            pltpu.VMEM((PIECES, PLANES, 2 * slots, width), BF16),
            pltpu.VMEM((PIECES, 4, slots, width), BF16),
            pltpu.VMEM((PIECES, 4, slots, width), BF16),
            pltpu.VMEM((PLANES, DEPTH, width), F32),
            pltpu.VMEM((PIECES, 2 * DEPTH, width), F32),
            pltpu.VMEM((PIECES, 2, DEPTH, width), F32),
            pltpu.VMEM((PIECES, 2, DEPTH, width), F32),
            pltpu.VMEM((PIECES, DEPTH, width), F32),
            pltpu.VMEM((PIECES, DEPTH, width), F32),
            pltpu.VMEM((2, slots, 2 * slots), F32),
            pltpu.VMEM((2, slots, 2 * slots), F32),
            pltpu.VMEM((2, 2 * slots, slots), F32),
            pltpu.SemaphoreType.DMA((PIECES,)),
            pair,
            pair,
            pair,
            pair,
            pair,
            pltpu.SemaphoreType.DMA((2, 2)),
            pltpu.SemaphoreType.DMA,
        ],
        compiler_params=pltpu.CompilerParams(
            collective_id=1, has_side_effects=True, vmem_limit_bytes=56 * 2**20
        ),
        cost_estimate=pl.CostEstimate(
            flops=4 * 10**9, bytes_accessed=5 * 2**20, transcendentals=2**16
        ),
    )(
        basis_wavefunctions.reshape(slots * depth, points),
        filling_weights.reshape(1, slots),
        living_per_unit,
        starting_sheets.reshape(count, slots),
        nucleus_charge,
        applied_field,
    )


def per_device(
    basis_wavefunctions,
    filling_weights,
    living_per_unit,
    starting_sheets,
    nucleus_charge,
    applied_field,
):
    slots, depth, points = basis_wavefunctions.shape
    count = lax.axis_size("func")
    width = points // PIECES
    anywhere = pl.BlockSpec(memory_space=pl.ANY)
    pair = pltpu.SemaphoreType.DMA((2, PIECES))
    rho, own, side, part_in, back, over = pl.pallas_call(
        functools.partial(packed_kernel, count),
        out_shape=(
            jax.ShapeDtypeStruct((depth, points), F32),
            jax.ShapeDtypeStruct((slots, 2 * slots), F32),
            jax.ShapeDtypeStruct((2, 2 * slots, slots), F32),
            jax.ShapeDtypeStruct((2, PARTS, 2 * slots), F32),
            jax.ShapeDtypeStruct((2, slots, slots), BF16),
            jax.ShapeDtypeStruct((1,), F32),
        ),
        in_specs=[anywhere] * 6,
        out_specs=(anywhere,) * 5 + (pl.BlockSpec(memory_space=pltpu.SMEM),),
        scratch_shapes=[
            pltpu.VMEM((PIECES, slots * depth, width), BF16),
            pltpu.VMEM((1, slots), F32),
            pltpu.VMEM((1, count), jnp.int32),
            pltpu.VMEM((count, slots), jnp.int32),
            pltpu.VMEM((depth, points), F32),
            pltpu.VMEM((depth, points), F32),
            pltpu.VMEM((count, slots), F32),
            pltpu.VMEM((GROUPS, PLANES * GROUP, slots), BF16),
            pltpu.VMEM((slots, slots), F32),
            pltpu.VMEM((2, slots, slots), BF16),
            pltpu.VMEM((2, slots, slots), BF16),
            pltpu.VMEM((PIECES, PLANES, 2 * slots, width), BF16),
            pltpu.VMEM((PIECES, MANY, width), BF16),
            pltpu.VMEM((PIECES, MANY, width), BF16),
            pltpu.VMEM((PIECES, MANY, width), BF16),
            pltpu.VMEM((PIECES, MANY, width), BF16),
            pltpu.VMEM((PIECES, 2 * DEPTH, width), F32),
            pltpu.VMEM((depth, points), F32),
            pltpu.VMEM((PIECES, DEPTH, width), F32),
            pltpu.VMEM((PIECES, 2 * DEPTH, width), BF16),
            pltpu.VMEM((PIECES, 2 * DEPTH, width), BF16),
            pltpu.VMEM((PIECES, DEPTH, width), F32),
            pltpu.VMEM((PIECES, DEPTH, width), F32),
            pltpu.VMEM((slots, 2 * slots), F32),
            pltpu.VMEM((2, slots, 2 * slots), F32),
            pltpu.VMEM((2, 2 * slots, slots), F32),
            pltpu.SemaphoreType.DMA((PIECES,)),
            pltpu.SemaphoreType.DMA((5,)),
            pair,
            pair,
            pair,
            pair,
            pltpu.SemaphoreType.DMA((2, 2)),
            pltpu.SemaphoreType.DMA((4,)),
        ],
        compiler_params=pltpu.CompilerParams(
            collective_id=0, has_side_effects=True, vmem_limit_bytes=56 * 2**20
        ),
        cost_estimate=pl.CostEstimate(
            flops=4 * 10**9, bytes_accessed=5 * 2**20, transcendentals=2**16
        ),
    )(
        basis_wavefunctions.reshape(slots * depth, points),
        filling_weights.reshape(1, slots),
        living_per_unit.reshape(1, count),
        starting_sheets.reshape(count, slots),
        nucleus_charge,
        applied_field,
    )

    def as_sent():
        return side, part_in

    def in_full():
        whole = full_call(
            basis_wavefunctions,
            filling_weights,
            living_per_unit,
            starting_sheets,
            nucleus_charge,
            applied_field,
        )
        return whole, jnp.zeros_like(part_in)

    side_blocks, received = lax.cond(over[0] > 0.0, in_full, as_sent)
    return tuple(
        pl.pallas_call(
            functools.partial(finish_kernel, 1.0 / (depth * points)),
            out_shape=(
                jax.ShapeDtypeStruct((depth, points), F32),
                jax.ShapeDtypeStruct((slots, 3 * slots), F32),
                jax.ShapeDtypeStruct((slots, 3 * slots), F32),
            ),
        )(rho, own, side_blocks, received, back)
    )


def solution(mesh):
    return jax.shard_map(
        per_device,
        mesh=mesh,
        in_specs=(P("func", None, None), P("func"), P(), P(), P("func", None), P("func", None)),
        out_specs=(P("func", None), P("func", None), P("func", None)),
        check_vma=False,
    )
```

```python
import functools

import jax
import jax.numpy as jnp
from jax import lax
from jax.experimental import pallas as pl
from jax.experimental.pallas import tpu as pltpu
from jax.sharding import PartitionSpec as P

MESH = pl.DeviceIdType.MESH
F32 = jnp.float32
BF16 = jnp.bfloat16

SLOTS = 128
DEPTH = 8
PLANES = 2 * DEPTH - 1
GROUP = 16
GROUPS = SLOTS // GROUP
PIECES = 4
LEVELS = 4
ROOM = (32, 64, 80, 96)
FIRST = (0, 32, 96, 176)
FEW, MANY = 176, 272
PARTS = 96
LAYERS = 4
UP_PIECES = 1


def dot_nt(a, b):
    return lax.dot_general(a, b, (((1,), (1,)), ((), ())), preferred_element_type=F32)


def cube_root(x):
    y = jnp.exp(jnp.log(x) * (1.0 / 3.0))
    return (2.0 * y + x / (y * y)) * (1.0 / 3.0)


def dot_nn(a, b):
    return lax.dot_general(a, b, (((1,), (0,)), ((), ())), preferred_element_type=F32)


def select_rows(one_hot, values):
    high = values.astype(BF16)
    low = (values - high.astype(F32)).astype(BF16)
    return dot_nn(one_hot, high) + dot_nn(one_hot, low)


def select_columns(values, one_hot):
    high = values.astype(BF16)
    low = (values - high.astype(F32)).astype(BF16)
    return dot_nn(high, one_hot) + dot_nn(low, one_hot)


def rank_matrix(key):
    row = lax.broadcasted_iota(jnp.int32, (SLOTS, SLOTS), 0)
    column = lax.broadcasted_iota(jnp.int32, (SLOTS, SLOTS), 1)
    wide = jnp.broadcast_to(key, (SLOTS, SLOTS))
    tall = wide.T
    before = jnp.where((tall < wide) | ((tall == wide) & (row < column)), 1.0, 0.0)
    rank = jnp.sum(before, axis=0, keepdims=True)
    return jnp.where(row.astype(F32) == rank, 1.0, 0.0)


def packed_kernel(
    count,
    boxes,
    weights_in,
    living_in,
    sheets_in,
    nucleus_in,
    applied_in,
    rho_out,
    own_out,
    side_out,
    part_in,
    back_out,
    over_out,
    raw,
    weights,
    living,
    sheets,
    nucleus,
    applied,
    starts,
    selector,
    wide_weights,
    order,
    back,
    stack,
    to_prev,
    to_next,
    from_prev,
    from_next,
    pot,
    rho,
    base,
    up_out,
    up_in,
    down_out,
    down_in,
    own,
    part,
    side,
    raw_sem,
    in_sems,
    down_sems,
    up_sems,
    planes_down_sems,
    planes_up_sems,
    part_sems,
    out_sems,
):
    me = lax.axis_index("func")
    following = lax.rem(me + 1, count)
    preceding = lax.rem(me + count - 1, count)
    width = raw.shape[2]
    step = min(width, 256)

    def points(piece):
        return pl.ds(pl.multiple_of(piece * width, width), width)

    def raw_copy(piece):
        return pltpu.make_async_copy(
            boxes.at[:, points(piece)], raw.at[piece], raw_sem.at[piece]
        )

    small = [
        pltpu.make_async_copy(source, target, in_sems.at[place])
        for place, (source, target) in enumerate(
            (
                (sheets_in, sheets),
                (living_in, living),
                (weights_in, weights),
                (nucleus_in, nucleus),
                (applied_in, applied),
            )
        )
    ]
    for copy in small:
        copy.start()
    for piece in range(PIECES):
        raw_copy(piece).start()

    barrier = pltpu.get_barrier_semaphore()
    for neighbour in (preceding, following):
        pl.semaphore_signal(barrier, inc=1, device_id=(neighbour,), device_id_type=MESH)
    for copy in small:
        copy.wait()

    alive = jnp.broadcast_to(living[...], (SLOTS, count)).T
    lane = lax.broadcasted_iota(jnp.int32, (count, SLOTS), 1)
    owner = lax.broadcasted_iota(jnp.int32, (count, SLOTS), 0)
    starts[...] = jnp.where(lane < alive, sheets[...] - owner * DEPTH, 64).astype(F32)

    start = starts[pl.ds(me, 1), :]
    lanes = lax.broadcasted_iota(jnp.int32, (GROUPS, SLOTS), 1)
    rows = lax.broadcasted_iota(jnp.int32, (GROUPS, SLOTS), 0)
    spread = jnp.where(lanes // GROUP == rows, start, 0.0).astype(BF16)
    repeat = (
        lax.broadcasted_iota(jnp.int32, (SLOTS, SLOTS), 0) % GROUP
        == lax.broadcasted_iota(jnp.int32, (SLOTS, SLOTS), 1) // DEPTH
    )
    column_start = dot_nn(spread, jnp.where(repeat, 1.0, 0.0).astype(BF16))
    row = lax.broadcasted_iota(jnp.int32, (PLANES * GROUP, SLOTS), 0)
    column = lax.broadcasted_iota(jnp.int32, (PLANES * GROUP, SLOTS), 1)
    offset = jnp.where(
        row % GROUP == column // DEPTH, row // GROUP - column % DEPTH, -99
    ).astype(F32)
    for group in range(GROUPS):
        selector[group] = jnp.where(offset == column_start[group : group + 1, :], 1.0, 0.0).astype(BF16)
    wide_weights[...] = jnp.broadcast_to(weights[...], (SLOTS, SLOTS)).T

    def up_matrix(device):
        return rank_matrix(starts[pl.ds(device, 1), :])

    def down_matrix(device):
        first = starts[pl.ds(device, 1), :]
        return rank_matrix(jnp.where(first < 64.0, -first, first))

    up_order = up_matrix(me)
    down_order = down_matrix(me)
    order[0] = up_order.astype(BF16)
    order[1] = down_order.astype(BF16)
    back[0] = up_order.T.astype(BF16)
    back[1] = down_order.T.astype(BF16)

    def down_copy(piece):
        return pltpu.make_async_remote_copy(
            src_ref=down_out.at[piece],
            dst_ref=down_in.at[piece],
            send_sem=down_sems.at[0, piece],
            recv_sem=down_sems.at[1, piece],
            device_id=(following,),
            device_id_type=MESH,
        )

    def up_copy(piece):
        return pltpu.make_async_remote_copy(
            src_ref=up_out.at[piece],
            dst_ref=up_in.at[piece],
            send_sem=up_sems.at[0, piece],
            recv_sem=up_sems.at[1, piece],
            device_id=(preceding,),
            device_id_type=MESH,
        )

    def planes_down_copy(piece, length):
        return pltpu.make_async_remote_copy(
            src_ref=to_next.at[piece, pl.ds(0, length)],
            dst_ref=from_prev.at[piece, pl.ds(0, length)],
            send_sem=planes_down_sems.at[0, piece],
            recv_sem=planes_down_sems.at[1, piece],
            device_id=(following,),
            device_id_type=MESH,
        )

    def planes_up_copy(piece, length):
        return pltpu.make_async_remote_copy(
            src_ref=to_prev.at[piece, pl.ds(0, length)],
            dst_ref=from_next.at[piece, pl.ds(0, length)],
            send_sem=planes_up_sems.at[0, piece],
            recv_sem=planes_up_sems.at[1, piece],
            device_id=(preceding,),
            device_id_type=MESH,
        )

    def place(piece):
        raw_copy(piece).wait()
        for part_of in range(width // step):
            columns = pl.ds(part_of * step, step)
            columns_of_all = pl.ds(pl.multiple_of(piece * width + part_of * step, step), step)
            dens = jnp.zeros((PLANES, DEPTH, step), F32)
            for group in range(GROUPS):
                source = raw[piece, group * GROUP * DEPTH : (group + 1) * GROUP * DEPTH, columns]
                placed = dot_nn(selector[group], source).reshape(PLANES, GROUP, step)
                stack[piece, :, group * GROUP : (group + 1) * GROUP, columns] = placed.astype(BF16)
                weight = wide_weights[group * GROUP : (group + 1) * GROUP, :]
                weight = jnp.concatenate([weight] * (step // SLOTS), axis=1)
                terms = placed * placed * weight[None]
                dens += terms[:, :DEPTH] + terms[:, DEPTH:]
            dens = jnp.sum(dens, axis=1)
            down_out[piece, : DEPTH - 1, columns] = dens[DEPTH:]
            down_out[piece, DEPTH - 1 :, columns] = jnp.zeros((1, step), F32)
            below = nucleus[:, columns_of_all] + dens[:DEPTH]
            base[piece, :, columns] = below
            up_out[piece, :DEPTH, columns] = below.astype(BF16)
            up_out[piece, DEPTH:, columns] = applied[:, columns_of_all].astype(BF16)

    def pack_up(piece, level):
        rows = pl.ds(FIRST[level], ROOM[level])
        to_prev[piece, rows, :] = dot_nn(
            order[0, : ROOM[level], :], stack[piece, level, :SLOTS, :]
        ).astype(BF16)

    def pack_down(piece, level):
        rows = pl.ds(FIRST[level], ROOM[level])
        to_next[piece, rows, :] = dot_nn(
            order[1, : ROOM[level], :], stack[piece, 2 * DEPTH - 2 - level, :SLOTS, :]
        ).astype(BF16)

    def pack(piece):
        for level in range(LEVELS - 1):
            pack_up(piece, level)
            pack_down(piece, level)

        @pl.when(piece < UP_PIECES)
        def _():
            pack_up(piece, LEVELS - 1)

        @pl.when(piece >= UP_PIECES)
        def _():
            pack_down(piece, LEVELS - 1)

    def send_density(piece):
        down_copy(piece).start()
        up_copy(piece).start()

    def send_planes(piece):
        @pl.when(piece < UP_PIECES)
        def _():
            planes_up_copy(piece, MANY).start()
            planes_down_copy(piece, FEW).start()

        @pl.when(piece >= UP_PIECES)
        def _():
            planes_up_copy(piece, FEW).start()
            planes_down_copy(piece, MANY).start()

    def place_and_pack(piece, carry):
        place(piece)
        pack(piece)
        return carry

    late = lax.rem(me, max(count // LAYERS, 1)) == 0
    place_and_pack(jnp.int32(0), 0)

    @pl.when(late)
    def _():
        lax.fori_loop(1, PIECES, place_and_pack, 0)

    pl.semaphore_wait(barrier, 2)
    send_density(jnp.int32(0))

    @pl.when(late)
    def _():
        for piece in range(1, PIECES):
            send_density(piece)

    send_planes(jnp.int32(0))

    def next_piece(piece, carry):
        @pl.when(jnp.logical_not(late))
        def _():
            place(piece)
            send_density(piece)
            pack(piece)

        send_planes(piece)
        return carry

    lax.fori_loop(1, PIECES, next_piece, 0)

    over = jnp.zeros((count, 1), F32)
    first = starts[...]
    for level in range(LEVELS):
        low = jnp.sum(jnp.where(first <= level, 1.0, 0.0), axis=1, keepdims=True)
        high = jnp.sum(
            jnp.where((first >= DEPTH - 1 - level) & (first < 64.0), 1.0, 0.0), axis=1, keepdims=True
        )
        over = jnp.maximum(over, jnp.maximum(low, high) - ROOM[level])
    over_out[0] = jnp.max(over)

    own[...] = jnp.zeros_like(own)

    def own_planes(piece, planes):
        overlap = own[:, :SLOTS]
        energy = own[:, SLOTS:]
        for plane in planes:
            phi = stack[piece, plane, :SLOTS, :]
            vphi = (phi.astype(F32) * pot[piece, plane : plane + 1, :]).astype(BF16)
            stack[piece, plane, SLOTS:, :] = vphi
            overlap += dot_nt(phi, phi)
            energy += dot_nt(phi, vphi)
        own[:, :SLOTS] = overlap
        own[:, SLOTS:] = energy

    def low_planes(piece, carry):
        down_copy(piece).wait_recv()
        density = base[piece] + down_in[piece]
        rho[:, points(piece)] = density
        pot[piece, :DEPTH] = applied[:, points(piece)] - 0.9847 * cube_root(density)
        own_planes(piece, range(DEPTH))
        return carry

    def high_planes(piece, carry):
        up_copy(piece).wait_recv()
        above = up_in[piece].astype(F32)
        pot[piece, DEPTH:] = above[DEPTH:] - 0.9847 * cube_root(above[:DEPTH] + down_out[piece])
        own_planes(piece, range(DEPTH, PLANES))
        return carry

    lax.fori_loop(0, PIECES, low_planes, 0)
    lax.fori_loop(0, PIECES, high_planes, 0)
    rho_copy = pltpu.make_async_copy(rho, rho_out, out_sems.at[0])
    own_copy = pltpu.make_async_copy(own, own_out, out_sems.at[1])
    back_copy = pltpu.make_async_copy(back, back_out, out_sems.at[2])
    rho_copy.start()
    own_copy.start()
    back_copy.start()

    part[...] = jnp.zeros_like(part)

    def cross_next(piece, level):
        return dot_nt(
            from_next[piece, FIRST[level] : FIRST[level] + ROOM[level], :],
            stack[piece, DEPTH + level],
        )

    def cross_prev(piece, level):
        return dot_nt(
            from_prev[piece, FIRST[level] : FIRST[level] + ROOM[level], :],
            stack[piece, DEPTH - 2 - level],
        )

    def add_levels(direction, products):
        edge = 0
        for level in range(LEVELS - 1):
            total = part[direction, edge : ROOM[level], :]
            for other in products[level:]:
                total += other[edge : ROOM[level]]
            part[direction, edge : ROOM[level], :] = total
            edge = ROOM[level]

    def cross_piece(piece, carry):
        @pl.when(piece < UP_PIECES)
        def _():
            planes_up_copy(piece, MANY).wait_recv()
            planes_down_copy(piece, FEW).wait_recv()
            part[0, : ROOM[LEVELS - 1], :] += cross_next(piece, LEVELS - 1)

        @pl.when(piece >= UP_PIECES)
        def _():
            planes_up_copy(piece, FEW).wait_recv()
            planes_down_copy(piece, MANY).wait_recv()
            part[1, : ROOM[LEVELS - 1], :] += cross_prev(piece, LEVELS - 1)

        with_next = [cross_next(piece, level) for level in range(LEVELS - 1)]
        with_prev = [cross_prev(piece, level) for level in range(LEVELS - 1)]
        add_levels(0, with_next)
        add_levels(1, with_prev)
        return carry

    lax.fori_loop(0, PIECES, cross_piece, 0)

    def part_copy(which, target):
        return pltpu.make_async_remote_copy(
            src_ref=part.at[which, pl.ds(0, PARTS)],
            dst_ref=part_in.at[which],
            send_sem=part_sems.at[0, which],
            recv_sem=part_sems.at[1, which],
            device_id=(target,),
            device_id_type=MESH,
        )

    part_to_next = part_copy(0, following)
    part_to_prev = part_copy(1, preceding)
    part_to_next.start()
    part_to_prev.start()
    side[0] = select_columns(part[0].T, up_matrix(following).astype(BF16))
    side[1] = select_columns(part[1].T, down_matrix(preceding).astype(BF16))
    side_copy = pltpu.make_async_copy(side, side_out, out_sems.at[3])
    side_copy.start()
    rho_copy.wait()
    own_copy.wait()
    back_copy.wait()
    side_copy.wait()
    for piece in range(PIECES):
        down_copy(piece).wait_send()
        up_copy(piece).wait_send()
        planes_up_copy(piece, MANY if piece < UP_PIECES else FEW).wait_send()
        planes_down_copy(piece, FEW if piece < UP_PIECES else MANY).wait_send()
    part_to_next.wait()
    part_to_prev.wait()


def finish_kernel(scale, side, part_in, rho, own, back, rho_out, ham_out, ovl_out):
    rho_out[...] = rho[...]
    none = jnp.zeros((SLOTS - PARTS, 2 * SLOTS), F32)
    from_prev = select_rows(back[0], jnp.concatenate([part_in[0], none], axis=0))
    from_next = select_rows(back[1], jnp.concatenate([part_in[1], none], axis=0))
    ovl_out[:, :SLOTS] = (side[1, :SLOTS, :] + from_prev[:, :SLOTS]) * scale
    ham_out[:, :SLOTS] = (side[1, SLOTS:, :] + from_prev[:, SLOTS:]) * scale
    ovl_out[:, SLOTS : 2 * SLOTS] = own[:, :SLOTS] * scale
    ham_out[:, SLOTS : 2 * SLOTS] = own[:, SLOTS:] * scale
    ovl_out[:, 2 * SLOTS :] = (side[0, :SLOTS, :] + from_next[:, :SLOTS]) * scale
    ham_out[:, 2 * SLOTS :] = (side[0, SLOTS:, :] + from_next[:, SLOTS:]) * scale


def full_kernel(
    count,
    boxes,
    weights,
    living,
    sheets,
    nucleus,
    applied,
    side_out,
    raw,
    selector,
    wide_weights,
    stack,
    from_prev,
    from_next,
    dens,
    pot,
    up_out,
    up_in,
    down_out,
    down_in,
    part,
    part_in,
    side,
    raw_sem,
    down_sems,
    up_sems,
    planes_down_sems,
    planes_up_sems,
    plane_sems,
    part_sems,
    out_sem,
):
    me = lax.axis_index("func")
    following = lax.rem(me + 1, count)
    preceding = lax.rem(me + count - 1, count)
    width = raw.shape[2]

    def points(piece):
        return pl.ds(pl.multiple_of(piece * width, width), width)

    def raw_copy(piece):
        return pltpu.make_async_copy(
            boxes.at[:, points(piece)], raw.at[piece], raw_sem.at[piece]
        )

    for piece in range(PIECES):
        raw_copy(piece).start()

    barrier = pltpu.get_barrier_semaphore()
    for neighbour in (preceding, following):
        pl.semaphore_signal(barrier, inc=1, device_id=(neighbour,), device_id_type=MESH)

    start = (sheets[pl.ds(me, 1), :] - me * DEPTH).astype(F32)
    lane = lax.broadcasted_iota(jnp.int32, (1, SLOTS), 1)
    start = jnp.where(lane < living[me], start, 64.0)
    lanes = lax.broadcasted_iota(jnp.int32, (GROUPS, SLOTS), 1)
    rows = lax.broadcasted_iota(jnp.int32, (GROUPS, SLOTS), 0)
    spread = jnp.where(lanes // GROUP == rows, start, 0.0).astype(BF16)
    repeat = (
        lax.broadcasted_iota(jnp.int32, (SLOTS, SLOTS), 0) % GROUP
        == lax.broadcasted_iota(jnp.int32, (SLOTS, SLOTS), 1) // DEPTH
    )
    column_start = jnp.dot(
        spread, jnp.where(repeat, 1.0, 0.0).astype(BF16), preferred_element_type=F32
    )
    row = lax.broadcasted_iota(jnp.int32, (PLANES * GROUP, SLOTS), 0)
    column = lax.broadcasted_iota(jnp.int32, (PLANES * GROUP, SLOTS), 1)
    offset = jnp.where(
        row % GROUP == column // DEPTH, row // GROUP - column % DEPTH, -99
    ).astype(F32)
    for group in range(GROUPS):
        selector[group] = jnp.where(offset == column_start[group : group + 1, :], 1.0, 0.0).astype(BF16)
    wide_weights[...] = jnp.broadcast_to(weights[...], (SLOTS, SLOTS)).T

    pl.semaphore_wait(barrier, 2)

    def down_copy(piece):
        return pltpu.make_async_remote_copy(
            src_ref=down_out.at[piece],
            dst_ref=down_in.at[piece],
            send_sem=down_sems.at[0, piece],
            recv_sem=down_sems.at[1, piece],
            device_id=(following,),
            device_id_type=MESH,
        )

    def up_copy(piece):
        return pltpu.make_async_remote_copy(
            src_ref=up_out.at[piece],
            dst_ref=up_in.at[piece],
            send_sem=up_sems.at[0, piece],
            recv_sem=up_sems.at[1, piece],
            device_id=(preceding,),
            device_id_type=MESH,
        )

    def planes_down_copy(piece):
        return pltpu.make_async_remote_copy(
            src_ref=stack.at[piece, pl.ds(DEPTH + 4, 3), pl.ds(0, SLOTS), :],
            dst_ref=from_prev.at[piece, pl.ds(1, 3)],
            send_sem=planes_down_sems.at[0, piece],
            recv_sem=planes_down_sems.at[1, piece],
            device_id=(following,),
            device_id_type=MESH,
        )

    def planes_up_copy(piece):
        return pltpu.make_async_remote_copy(
            src_ref=stack.at[piece, pl.ds(0, 3), pl.ds(0, SLOTS), :],
            dst_ref=from_next.at[piece, pl.ds(0, 3)],
            send_sem=planes_up_sems.at[0, piece],
            recv_sem=planes_up_sems.at[1, piece],
            device_id=(preceding,),
            device_id_type=MESH,
        )

    def plane_up_copy(piece):
        return pltpu.make_async_remote_copy(
            src_ref=stack.at[piece, 3, pl.ds(0, SLOTS), :],
            dst_ref=from_next.at[piece, 3],
            send_sem=plane_sems.at[0, piece],
            recv_sem=plane_sems.at[1, piece],
            device_id=(preceding,),
            device_id_type=MESH,
        )

    def plane_down_copy(piece):
        return pltpu.make_async_remote_copy(
            src_ref=stack.at[piece, DEPTH + 3, pl.ds(0, SLOTS), :],
            dst_ref=from_prev.at[piece, 0],
            send_sem=plane_sems.at[0, piece],
            recv_sem=plane_sems.at[1, piece],
            device_id=(following,),
            device_id_type=MESH,
        )

    def place_piece(piece, carry):
        raw_copy(piece).wait()
        dens[...] = jnp.zeros_like(dens)

        def place_group(group, carry):
            slots = pl.ds(pl.multiple_of(group * GROUP, GROUP), GROUP)
            source = raw[piece, pl.ds(pl.multiple_of(group * GROUP * DEPTH, GROUP * DEPTH), GROUP * DEPTH), :]
            placed = jnp.dot(selector[group], source, preferred_element_type=F32)
            placed = placed.reshape(PLANES, GROUP, width)
            stack[piece, :, slots, :] = placed.astype(BF16)
            weight = jnp.concatenate([wide_weights[slots, :]] * (width // SLOTS), axis=1)
            terms = placed * placed * weight[None]
            dens[...] += terms[:, :DEPTH] + terms[:, DEPTH:]
            return carry

        lax.fori_loop(0, GROUPS, place_group, 0)
        down_out[piece] = jnp.zeros_like(down_out[piece])
        down_out[piece, : DEPTH - 1] = jnp.sum(dens[DEPTH:], axis=1)
        up_out[piece, 0] = nucleus[:, points(piece)] + jnp.sum(dens[:DEPTH], axis=1)
        up_out[piece, 1] = applied[:, points(piece)]
        down_copy(piece).start()
        up_copy(piece).start()
        planes_down_copy(piece).start()
        planes_up_copy(piece).start()

        @pl.when(piece < PIECES // 2)
        def _():
            plane_up_copy(piece).start()

        @pl.when(piece >= PIECES // 2)
        def _():
            plane_down_copy(piece).start()

        return carry

    lax.fori_loop(0, PIECES, place_piece, 0)

    def own_piece(piece, carry):
        down_copy(piece).wait()
        up_copy(piece).wait()
        density = up_out[piece, 0] + down_in[piece]
        pot[piece, :DEPTH] = up_out[piece, 1] - 0.9847 * cube_root(density)
        pot[piece, DEPTH:] = up_in[piece, 1] - 0.9847 * cube_root(up_in[piece, 0] + down_out[piece])
        for plane in range(PLANES):
            phi = stack[piece, plane, :SLOTS, :]
            stack[piece, plane, SLOTS:, :] = (phi.astype(F32) * pot[piece, plane : plane + 1, :]).astype(BF16)
        return carry

    lax.fori_loop(0, PIECES, own_piece, 0)
    part[...] = jnp.zeros_like(part)

    def cross_piece(piece, carry):
        planes_up_copy(piece).wait()
        planes_down_copy(piece).wait()
        total = part[0]
        for shared in range(3):
            total += dot_nt(from_next[piece, shared], stack[piece, DEPTH + shared])
        part[0] = total
        total = part[1]
        for shared in range(4, 7):
            total += dot_nt(from_prev[piece, shared - 3], stack[piece, shared])
        part[1] = total

        @pl.when(piece < PIECES // 2)
        def _():
            plane_up_copy(piece).wait()
            part[0] += dot_nt(from_next[piece, 3], stack[piece, DEPTH + 3])

        @pl.when(piece >= PIECES // 2)
        def _():
            plane_down_copy(piece).wait()
            part[1] += dot_nt(from_prev[piece, 0], stack[piece, 3])

        return carry

    lax.fori_loop(0, PIECES, cross_piece, 0)

    def part_copy(side, target):
        return pltpu.make_async_remote_copy(
            src_ref=part.at[side],
            dst_ref=part_in.at[side],
            send_sem=part_sems.at[0, side],
            recv_sem=part_sems.at[1, side],
            device_id=(target,),
            device_id_type=MESH,
        )

    to_next = part_copy(0, following)
    to_prev = part_copy(1, preceding)
    to_next.start()
    to_prev.start()
    to_next.wait()
    to_prev.wait()
    side[0, :SLOTS] = part[0, :, :SLOTS].T + part_in[1, :, :SLOTS]
    side[0, SLOTS:] = part[0, :, SLOTS:].T + part_in[1, :, SLOTS:]
    side[1, :SLOTS] = part[1, :, :SLOTS].T + part_in[0, :, :SLOTS]
    side[1, SLOTS:] = part[1, :, SLOTS:].T + part_in[0, :, SLOTS:]
    side_copy = pltpu.make_async_copy(side, side_out, out_sem)
    side_copy.start()
    side_copy.wait()


def full_call(
    basis_wavefunctions,
    filling_weights,
    living_per_unit,
    starting_sheets,
    nucleus_charge,
    applied_field,
):
    slots, depth, points = basis_wavefunctions.shape
    count = lax.axis_size("func")
    width = points // PIECES
    vmem = pl.BlockSpec(memory_space=pltpu.VMEM)
    anywhere = pl.BlockSpec(memory_space=pl.ANY)
    pair = pltpu.SemaphoreType.DMA((2, PIECES))
    return pl.pallas_call(
        functools.partial(full_kernel, count),
        out_shape=jax.ShapeDtypeStruct((2, 2 * slots, slots), F32),
        in_specs=[
            anywhere,
            vmem,
            pl.BlockSpec(memory_space=pltpu.SMEM),
            vmem,
            vmem,
            vmem,
        ],
        out_specs=anywhere,
        scratch_shapes=[
            pltpu.VMEM((PIECES, slots * depth, width), BF16),
            pltpu.VMEM((GROUPS, PLANES * GROUP, slots), BF16),
            pltpu.VMEM((slots, slots), F32),
            pltpu.VMEM((PIECES, PLANES, 2 * slots, width), BF16),
            pltpu.VMEM((PIECES, 4, slots, width), BF16),
            pltpu.VMEM((PIECES, 4, slots, width), BF16),
            pltpu.VMEM((PLANES, DEPTH, width), F32),
            pltpu.VMEM((PIECES, 2 * DEPTH, width), F32),
            pltpu.VMEM((PIECES, 2, DEPTH, width), F32),
            pltpu.VMEM((PIECES, 2, DEPTH, width), F32),
            pltpu.VMEM((PIECES, DEPTH, width), F32),
            pltpu.VMEM((PIECES, DEPTH, width), F32),
            pltpu.VMEM((2, slots, 2 * slots), F32),
            pltpu.VMEM((2, slots, 2 * slots), F32),
            pltpu.VMEM((2, 2 * slots, slots), F32),
            pltpu.SemaphoreType.DMA((PIECES,)),
            pair,
            pair,
            pair,
            pair,
            pair,
            pltpu.SemaphoreType.DMA((2, 2)),
            pltpu.SemaphoreType.DMA,
        ],
        compiler_params=pltpu.CompilerParams(
            collective_id=1, has_side_effects=True, vmem_limit_bytes=56 * 2**20
        ),
        cost_estimate=pl.CostEstimate(
            flops=4 * 10**9, bytes_accessed=5 * 2**20, transcendentals=2**16
        ),
    )(
        basis_wavefunctions.reshape(slots * depth, points),
        filling_weights.reshape(1, slots),
        living_per_unit,
        starting_sheets.reshape(count, slots),
        nucleus_charge,
        applied_field,
    )


def per_device(
    basis_wavefunctions,
    filling_weights,
    living_per_unit,
    starting_sheets,
    nucleus_charge,
    applied_field,
):
    slots, depth, points = basis_wavefunctions.shape
    count = lax.axis_size("func")
    width = points // PIECES
    anywhere = pl.BlockSpec(memory_space=pl.ANY)
    pair = pltpu.SemaphoreType.DMA((2, PIECES))
    rho, own, side, part_in, back, over = pl.pallas_call(
        functools.partial(packed_kernel, count),
        out_shape=(
            jax.ShapeDtypeStruct((depth, points), F32),
            jax.ShapeDtypeStruct((slots, 2 * slots), F32),
            jax.ShapeDtypeStruct((2, 2 * slots, slots), F32),
            jax.ShapeDtypeStruct((2, PARTS, 2 * slots), F32),
            jax.ShapeDtypeStruct((2, slots, slots), BF16),
            jax.ShapeDtypeStruct((1,), F32),
        ),
        in_specs=[anywhere] * 6,
        out_specs=(anywhere,) * 5 + (pl.BlockSpec(memory_space=pltpu.SMEM),),
        scratch_shapes=[
            pltpu.VMEM((PIECES, slots * depth, width), BF16),
            pltpu.VMEM((1, slots), F32),
            pltpu.VMEM((1, count), jnp.int32),
            pltpu.VMEM((count, slots), jnp.int32),
            pltpu.VMEM((depth, points), F32),
            pltpu.VMEM((depth, points), F32),
            pltpu.VMEM((count, slots), F32),
            pltpu.VMEM((GROUPS, PLANES * GROUP, slots), BF16),
            pltpu.VMEM((slots, slots), F32),
            pltpu.VMEM((2, slots, slots), BF16),
            pltpu.VMEM((2, slots, slots), BF16),
            pltpu.VMEM((PIECES, PLANES, 2 * slots, width), BF16),
            pltpu.VMEM((PIECES, MANY, width), BF16),
            pltpu.VMEM((PIECES, MANY, width), BF16),
            pltpu.VMEM((PIECES, MANY, width), BF16),
            pltpu.VMEM((PIECES, MANY, width), BF16),
            pltpu.VMEM((PIECES, 2 * DEPTH, width), F32),
            pltpu.VMEM((depth, points), F32),
            pltpu.VMEM((PIECES, DEPTH, width), F32),
            pltpu.VMEM((PIECES, 2 * DEPTH, width), BF16),
            pltpu.VMEM((PIECES, 2 * DEPTH, width), BF16),
            pltpu.VMEM((PIECES, DEPTH, width), F32),
            pltpu.VMEM((PIECES, DEPTH, width), F32),
            pltpu.VMEM((slots, 2 * slots), F32),
            pltpu.VMEM((2, slots, 2 * slots), F32),
            pltpu.VMEM((2, 2 * slots, slots), F32),
            pltpu.SemaphoreType.DMA((PIECES,)),
            pltpu.SemaphoreType.DMA((5,)),
            pair,
            pair,
            pair,
            pair,
            pltpu.SemaphoreType.DMA((2, 2)),
            pltpu.SemaphoreType.DMA((4,)),
        ],
        compiler_params=pltpu.CompilerParams(
            collective_id=0, has_side_effects=True, vmem_limit_bytes=56 * 2**20
        ),
        cost_estimate=pl.CostEstimate(
            flops=4 * 10**9, bytes_accessed=5 * 2**20, transcendentals=2**16
        ),
    )(
        basis_wavefunctions.reshape(slots * depth, points),
        filling_weights.reshape(1, slots),
        living_per_unit.reshape(1, count),
        starting_sheets.reshape(count, slots),
        nucleus_charge,
        applied_field,
    )

    def as_sent():
        return side, part_in, rho, own, back

    def in_full():
        whole = full_call(
            basis_wavefunctions,
            filling_weights,
            living_per_unit,
            starting_sheets,
            nucleus_charge,
            applied_field,
        )
        return whole, jnp.zeros_like(part_in), rho, own, back

    given = lax.cond(over[0] > 0.0, in_full, as_sent)
    return tuple(
        pl.pallas_call(
            functools.partial(finish_kernel, 1.0 / (depth * points)),
            out_shape=(
                jax.ShapeDtypeStruct((depth, points), F32),
                jax.ShapeDtypeStruct((slots, 3 * slots), F32),
                jax.ShapeDtypeStruct((slots, 3 * slots), F32),
            ),
        )(*given)
    )


def solution(mesh):
    return jax.shard_map(
        per_device,
        mesh=mesh,
        in_specs=(P("func", None, None), P("func"), P(), P(), P("func", None), P("func", None)),
        out_specs=(P("func", None), P("func", None), P("func", None)),
        check_vma=False,
    )
```

```python
import functools

import jax
import jax.numpy as jnp
from jax import lax
from jax.experimental import pallas as pl
from jax.experimental.pallas import tpu as pltpu
from jax.sharding import PartitionSpec as P

MESH = pl.DeviceIdType.MESH
F32 = jnp.float32
BF16 = jnp.bfloat16

SLOTS = 128
DEPTH = 8
PLANES = 2 * DEPTH - 1
GROUP = 16
GROUPS = SLOTS // GROUP
PIECES = 4
LEVELS = 4
ROOM = (32, 64, 80, 96)
FIRST = (0, 32, 96, 176)
FEW, MANY = 176, 272
PARTS = (80, 96)
LAYERS = 4
UP_PIECES = 0


def dot_nt(a, b):
    return lax.dot_general(a, b, (((1,), (1,)), ((), ())), preferred_element_type=F32)


def cube_root(x):
    y = jnp.exp(jnp.log(x) * (1.0 / 3.0))
    return (2.0 * y + x / (y * y)) * (1.0 / 3.0)


def dot_nn(a, b):
    return lax.dot_general(a, b, (((1,), (0,)), ((), ())), preferred_element_type=F32)


def select_rows(one_hot, values):
    high = values.astype(BF16)
    low = (values - high.astype(F32)).astype(BF16)
    return dot_nn(one_hot, high) + dot_nn(one_hot, low)


def select_columns(values, one_hot):
    high = values.astype(BF16)
    low = (values - high.astype(F32)).astype(BF16)
    return dot_nn(high, one_hot) + dot_nn(low, one_hot)


def rank_matrix(key):
    row = lax.broadcasted_iota(jnp.int32, (SLOTS, SLOTS), 0)
    column = lax.broadcasted_iota(jnp.int32, (SLOTS, SLOTS), 1)
    wide = jnp.broadcast_to(key, (SLOTS, SLOTS))
    tall = wide.T
    before = jnp.where((tall < wide) | ((tall == wide) & (row < column)), 1.0, 0.0)
    rank = jnp.sum(before, axis=0, keepdims=True)
    return jnp.where(row.astype(F32) == rank, 1.0, 0.0)


def packed_kernel(
    count,
    boxes,
    weights_in,
    living_in,
    sheets_in,
    nucleus_in,
    applied_in,
    rho_out,
    own_out,
    side_out,
    part_in,
    back_out,
    over_out,
    raw,
    weights,
    living,
    sheets,
    nucleus,
    applied,
    starts,
    selector,
    wide_weights,
    order,
    back,
    stack,
    to_prev,
    to_next,
    from_prev,
    from_next,
    pot,
    rho,
    base,
    up_out,
    up_in,
    down_out,
    down_in,
    own,
    part,
    side,
    raw_sem,
    in_sems,
    down_sems,
    up_sems,
    planes_down_sems,
    planes_up_sems,
    part_sems,
    out_sems,
):
    me = lax.axis_index("func")
    following = lax.rem(me + 1, count)
    preceding = lax.rem(me + count - 1, count)
    barrier = pltpu.get_barrier_semaphore()
    for neighbour in (preceding, following):
        pl.semaphore_signal(barrier, inc=1, device_id=(neighbour,), device_id_type=MESH)
    width = raw.shape[2]
    step = min(width, 256)

    def points(piece):
        return pl.ds(pl.multiple_of(piece * width, width), width)

    def raw_copy(piece):
        return pltpu.make_async_copy(
            boxes.at[:, points(piece)], raw.at[piece], raw_sem.at[piece]
        )

    small = [
        pltpu.make_async_copy(source, target, in_sems.at[place])
        for place, (source, target) in enumerate(
            (
                (sheets_in, sheets),
                (living_in, living),
                (weights_in, weights),
                (nucleus_in, nucleus),
                (applied_in, applied),
            )
        )
    ]
    for copy in small:
        copy.start()
    for piece in range(PIECES):
        raw_copy(piece).start()

    for copy in small:
        copy.wait()

    alive = jnp.broadcast_to(living[...], (SLOTS, count)).T
    lane = lax.broadcasted_iota(jnp.int32, (count, SLOTS), 1)
    owner = lax.broadcasted_iota(jnp.int32, (count, SLOTS), 0)
    starts[...] = jnp.where(lane < alive, sheets[...] - owner * DEPTH, 64).astype(F32)

    start = starts[pl.ds(me, 1), :]
    lanes = lax.broadcasted_iota(jnp.int32, (GROUPS, SLOTS), 1)
    rows = lax.broadcasted_iota(jnp.int32, (GROUPS, SLOTS), 0)
    spread = jnp.where(lanes // GROUP == rows, start, 0.0).astype(BF16)
    repeat = (
        lax.broadcasted_iota(jnp.int32, (SLOTS, SLOTS), 0) % GROUP
        == lax.broadcasted_iota(jnp.int32, (SLOTS, SLOTS), 1) // DEPTH
    )
    column_start = dot_nn(spread, jnp.where(repeat, 1.0, 0.0).astype(BF16))
    row = lax.broadcasted_iota(jnp.int32, (PLANES * GROUP, SLOTS), 0)
    column = lax.broadcasted_iota(jnp.int32, (PLANES * GROUP, SLOTS), 1)
    offset = jnp.where(
        row % GROUP == column // DEPTH, row // GROUP - column % DEPTH, -99
    ).astype(F32)
    for group in range(GROUPS):
        selector[group] = jnp.where(offset == column_start[group : group + 1, :], 1.0, 0.0).astype(BF16)
    wide_weights[...] = jnp.broadcast_to(weights[...], (SLOTS, SLOTS)).T

    def up_matrix(device):
        return rank_matrix(starts[pl.ds(device, 1), :])

    def down_matrix(device):
        first = starts[pl.ds(device, 1), :]
        return rank_matrix(jnp.where(first < 64.0, -first, first))

    up_order = up_matrix(me)
    down_order = down_matrix(me)
    order[0] = up_order.astype(BF16)
    order[1] = down_order.astype(BF16)
    back[0] = up_order.T.astype(BF16)
    back[1] = down_order.T.astype(BF16)

    def down_copy(piece):
        return pltpu.make_async_remote_copy(
            src_ref=down_out.at[piece],
            dst_ref=down_in.at[piece],
            send_sem=down_sems.at[0, piece],
            recv_sem=down_sems.at[1, piece],
            device_id=(following,),
            device_id_type=MESH,
        )

    def up_copy(piece):
        return pltpu.make_async_remote_copy(
            src_ref=up_out.at[piece],
            dst_ref=up_in.at[piece],
            send_sem=up_sems.at[0, piece],
            recv_sem=up_sems.at[1, piece],
            device_id=(preceding,),
            device_id_type=MESH,
        )

    def planes_down_copy(piece, length):
        return pltpu.make_async_remote_copy(
            src_ref=to_next.at[piece, pl.ds(0, length)],
            dst_ref=from_prev.at[piece, pl.ds(0, length)],
            send_sem=planes_down_sems.at[0, piece],
            recv_sem=planes_down_sems.at[1, piece],
            device_id=(following,),
            device_id_type=MESH,
        )

    def planes_up_copy(piece, length):
        return pltpu.make_async_remote_copy(
            src_ref=to_prev.at[piece, pl.ds(0, length)],
            dst_ref=from_next.at[piece, pl.ds(0, length)],
            send_sem=planes_up_sems.at[0, piece],
            recv_sem=planes_up_sems.at[1, piece],
            device_id=(preceding,),
            device_id_type=MESH,
        )

    def place(piece):
        raw_copy(piece).wait()
        for part_of in range(width // step):
            columns = pl.ds(part_of * step, step)
            columns_of_all = pl.ds(pl.multiple_of(piece * width + part_of * step, step), step)
            dens = jnp.zeros((PLANES, DEPTH, step), F32)
            for group in range(GROUPS):
                source = raw[piece, group * GROUP * DEPTH : (group + 1) * GROUP * DEPTH, columns]
                placed = dot_nn(selector[group], source).reshape(PLANES, GROUP, step)
                stack[piece, :, group * GROUP : (group + 1) * GROUP, columns] = placed.astype(BF16)
                weight = wide_weights[group * GROUP : (group + 1) * GROUP, :]
                weight = jnp.concatenate([weight] * (step // SLOTS), axis=1)
                terms = placed * placed * weight[None]
                dens += terms[:, :DEPTH] + terms[:, DEPTH:]
            dens = jnp.sum(dens, axis=1)
            down_out[piece, : DEPTH - 1, columns] = dens[DEPTH:]
            down_out[piece, DEPTH - 1 :, columns] = jnp.zeros((1, step), F32)
            below = nucleus[:, columns_of_all] + dens[:DEPTH]
            base[piece, :, columns] = below
            up_out[piece, :DEPTH, columns] = below.astype(BF16)
            up_out[piece, DEPTH:, columns] = applied[:, columns_of_all].astype(BF16)

    def pack_up(piece, level):
        rows = pl.ds(FIRST[level], ROOM[level])
        to_prev[piece, rows, :] = dot_nn(
            order[0, : ROOM[level], :], stack[piece, level, :SLOTS, :]
        ).astype(BF16)

    def pack_down(piece, level):
        rows = pl.ds(FIRST[level], ROOM[level])
        to_next[piece, rows, :] = dot_nn(
            order[1, : ROOM[level], :], stack[piece, 2 * DEPTH - 2 - level, :SLOTS, :]
        ).astype(BF16)

    def pack(piece):
        for level in range(LEVELS - 1):
            pack_up(piece, level)
            pack_down(piece, level)

        @pl.when(piece < UP_PIECES)
        def _():
            pack_up(piece, LEVELS - 1)

        @pl.when(piece >= UP_PIECES)
        def _():
            pack_down(piece, LEVELS - 1)

    def send_density(piece):
        down_copy(piece).start()
        up_copy(piece).start()

    def send_planes(piece):
        @pl.when(piece < UP_PIECES)
        def _():
            planes_up_copy(piece, MANY).start()
            planes_down_copy(piece, FEW).start()

        @pl.when(piece >= UP_PIECES)
        def _():
            planes_up_copy(piece, FEW).start()
            planes_down_copy(piece, MANY).start()

    def place_and_pack(piece, carry):
        place(piece)
        pack(piece)
        return carry

    late = lax.rem(me, max(count // LAYERS, 1)) == 0
    place_and_pack(jnp.int32(0), 0)

    @pl.when(late)
    def _():
        lax.fori_loop(1, PIECES, place_and_pack, 0)

    pl.semaphore_wait(barrier, 2)
    send_density(jnp.int32(0))

    @pl.when(late)
    def _():
        for piece in range(1, PIECES):
            send_density(piece)

    send_planes(jnp.int32(0))

    def next_piece(piece, carry):
        @pl.when(jnp.logical_not(late))
        def _():
            place(piece)
            send_density(piece)
            pack(piece)

        send_planes(piece)
        return carry

    lax.fori_loop(1, PIECES, next_piece, 0)

    over = jnp.zeros((count, 1), F32)
    first = starts[...]
    for level in range(LEVELS):
        low = jnp.sum(jnp.where(first <= level, 1.0, 0.0), axis=1, keepdims=True)
        high = jnp.sum(
            jnp.where((first >= DEPTH - 1 - level) & (first < 64.0), 1.0, 0.0), axis=1, keepdims=True
        )
        over = jnp.maximum(over, jnp.maximum(low, high) - ROOM[level])
    over_out[0] = jnp.max(over)

    own[...] = jnp.zeros_like(own)

    def own_planes(piece, planes):
        overlap = own[:, :SLOTS]
        energy = own[:, SLOTS:]
        for plane in planes:
            phi = stack[piece, plane, :SLOTS, :]
            vphi = (phi.astype(F32) * pot[piece, plane : plane + 1, :]).astype(BF16)
            stack[piece, plane, SLOTS:, :] = vphi
            overlap += dot_nt(phi, phi)
            energy += dot_nt(phi, vphi)
        own[:, :SLOTS] = overlap
        own[:, SLOTS:] = energy

    def low_planes(piece, carry):
        down_copy(piece).wait_recv()
        density = base[piece] + down_in[piece]
        rho[:, points(piece)] = density
        pot[piece, :DEPTH] = applied[:, points(piece)] - 0.9847 * cube_root(density)
        own_planes(piece, range(DEPTH))
        return carry

    def high_planes(piece, carry):
        up_copy(piece).wait_recv()
        above = up_in[piece].astype(F32)
        pot[piece, DEPTH:] = above[DEPTH:] - 0.9847 * cube_root(above[:DEPTH] + down_out[piece])
        own_planes(piece, range(DEPTH, PLANES))
        return carry

    part[...] = jnp.zeros_like(part)

    def cross_next(piece, level):
        return dot_nt(
            from_next[piece, FIRST[level] : FIRST[level] + ROOM[level], :],
            stack[piece, DEPTH + level],
        )

    def cross_prev(piece, level):
        return dot_nt(
            from_prev[piece, FIRST[level] : FIRST[level] + ROOM[level], :],
            stack[piece, DEPTH - 2 - level],
        )

    def add_levels(direction, products):
        edge = 0
        for level in range(LEVELS - 1):
            total = part[direction, edge : ROOM[level], :]
            for other in products[level:]:
                total += other[edge : ROOM[level]]
            part[direction, edge : ROOM[level], :] = total
            edge = ROOM[level]

    odd = lax.rem(me, 2) == 1

    def products_with_next(piece):
        @pl.when(piece < UP_PIECES)
        def _():
            planes_up_copy(piece, MANY).wait_recv()
            part[0, : ROOM[LEVELS - 1], :] += cross_next(piece, LEVELS - 1)

        @pl.when(piece >= UP_PIECES)
        def _():
            planes_up_copy(piece, FEW).wait_recv()

        add_levels(0, [cross_next(piece, level) for level in range(LEVELS - 1)])

    def products_with_previous(piece):
        @pl.when(piece < UP_PIECES)
        def _():
            planes_down_copy(piece, FEW).wait_recv()

        @pl.when(piece >= UP_PIECES)
        def _():
            planes_down_copy(piece, MANY).wait_recv()
            part[1, : ROOM[LEVELS - 1], :] += cross_prev(piece, LEVELS - 1)

        add_levels(1, [cross_prev(piece, level) for level in range(LEVELS - 1)])

    def cross_piece(piece):
        @pl.when(odd)
        def _():
            products_with_previous(piece)
            products_with_next(piece)

        @pl.when(jnp.logical_not(odd))
        def _():
            products_with_next(piece)
            products_with_previous(piece)

    @pl.when(odd)
    def _():
        lax.fori_loop(0, PIECES, low_planes, 0)

    @pl.when(jnp.logical_not(odd))
    def _():
        lax.fori_loop(0, PIECES, high_planes, 0)

    def other_planes(piece, carry):
        @pl.when(odd)
        def _():
            high_planes(piece, 0)

        @pl.when(jnp.logical_not(odd))
        def _():
            low_planes(piece, 0)

        @pl.when(piece > 0)
        def _():
            cross_piece(piece - 1)

        return carry

    lax.fori_loop(0, PIECES, other_planes, 0)
    cross_piece(jnp.int32(PIECES - 1))

    def part_copy(which, target):
        return pltpu.make_async_remote_copy(
            src_ref=part.at[which, pl.ds(0, PARTS[which])],
            dst_ref=part_in.at[which, pl.ds(0, PARTS[which])],
            send_sem=part_sems.at[0, which],
            recv_sem=part_sems.at[1, which],
            device_id=(target,),
            device_id_type=MESH,
        )

    part_to_next = part_copy(0, following)
    part_to_prev = part_copy(1, preceding)
    part_to_next.start()
    part_to_prev.start()
    rho_copy = pltpu.make_async_copy(rho, rho_out, out_sems.at[0])
    own_copy = pltpu.make_async_copy(own, own_out, out_sems.at[1])
    back_copy = pltpu.make_async_copy(back, back_out, out_sems.at[2])
    rho_copy.start()
    own_copy.start()
    back_copy.start()
    side[0] = select_columns(part[0].T, up_matrix(following).astype(BF16))
    side[1] = select_columns(part[1].T, down_matrix(preceding).astype(BF16))
    side_copy = pltpu.make_async_copy(side, side_out, out_sems.at[3])
    side_copy.start()
    rho_copy.wait()
    own_copy.wait()
    back_copy.wait()
    side_copy.wait()
    for piece in range(PIECES):
        down_copy(piece).wait_send()
        up_copy(piece).wait_send()
        planes_up_copy(piece, MANY if piece < UP_PIECES else FEW).wait_send()
        planes_down_copy(piece, FEW if piece < UP_PIECES else MANY).wait_send()
    part_to_next.wait()
    part_to_prev.wait()


def finish_kernel(scale, side, part_in, rho, own, back, rho_out, ham_out, ovl_out):
    rho_out[...] = rho[...]

    def rows_of(which):
        none = jnp.zeros((SLOTS - PARTS[which], 2 * SLOTS), F32)
        return select_rows(back[which], jnp.concatenate([part_in[which, : PARTS[which]], none], axis=0))

    from_prev = rows_of(0)
    from_next = rows_of(1)
    ovl_out[:, :SLOTS] = (side[1, :SLOTS, :] + from_prev[:, :SLOTS]) * scale
    ham_out[:, :SLOTS] = (side[1, SLOTS:, :] + from_prev[:, SLOTS:]) * scale
    ovl_out[:, SLOTS : 2 * SLOTS] = own[:, :SLOTS] * scale
    ham_out[:, SLOTS : 2 * SLOTS] = own[:, SLOTS:] * scale
    ovl_out[:, 2 * SLOTS :] = (side[0, :SLOTS, :] + from_next[:, :SLOTS]) * scale
    ham_out[:, 2 * SLOTS :] = (side[0, SLOTS:, :] + from_next[:, SLOTS:]) * scale


def full_kernel(
    count,
    boxes,
    weights,
    living,
    sheets,
    nucleus,
    applied,
    side_out,
    raw,
    selector,
    wide_weights,
    stack,
    from_prev,
    from_next,
    dens,
    pot,
    up_out,
    up_in,
    down_out,
    down_in,
    part,
    part_in,
    side,
    raw_sem,
    down_sems,
    up_sems,
    planes_down_sems,
    planes_up_sems,
    plane_sems,
    part_sems,
    out_sem,
):
    me = lax.axis_index("func")
    following = lax.rem(me + 1, count)
    preceding = lax.rem(me + count - 1, count)
    width = raw.shape[2]

    def points(piece):
        return pl.ds(pl.multiple_of(piece * width, width), width)

    def raw_copy(piece):
        return pltpu.make_async_copy(
            boxes.at[:, points(piece)], raw.at[piece], raw_sem.at[piece]
        )

    for piece in range(PIECES):
        raw_copy(piece).start()

    barrier = pltpu.get_barrier_semaphore()
    for neighbour in (preceding, following):
        pl.semaphore_signal(barrier, inc=1, device_id=(neighbour,), device_id_type=MESH)

    start = (sheets[pl.ds(me, 1), :] - me * DEPTH).astype(F32)
    lane = lax.broadcasted_iota(jnp.int32, (1, SLOTS), 1)
    start = jnp.where(lane < living[me], start, 64.0)
    lanes = lax.broadcasted_iota(jnp.int32, (GROUPS, SLOTS), 1)
    rows = lax.broadcasted_iota(jnp.int32, (GROUPS, SLOTS), 0)
    spread = jnp.where(lanes // GROUP == rows, start, 0.0).astype(BF16)
    repeat = (
        lax.broadcasted_iota(jnp.int32, (SLOTS, SLOTS), 0) % GROUP
        == lax.broadcasted_iota(jnp.int32, (SLOTS, SLOTS), 1) // DEPTH
    )
    column_start = jnp.dot(
        spread, jnp.where(repeat, 1.0, 0.0).astype(BF16), preferred_element_type=F32
    )
    row = lax.broadcasted_iota(jnp.int32, (PLANES * GROUP, SLOTS), 0)
    column = lax.broadcasted_iota(jnp.int32, (PLANES * GROUP, SLOTS), 1)
    offset = jnp.where(
        row % GROUP == column // DEPTH, row // GROUP - column % DEPTH, -99
    ).astype(F32)
    for group in range(GROUPS):
        selector[group] = jnp.where(offset == column_start[group : group + 1, :], 1.0, 0.0).astype(BF16)
    wide_weights[...] = jnp.broadcast_to(weights[...], (SLOTS, SLOTS)).T

    pl.semaphore_wait(barrier, 2)

    def down_copy(piece):
        return pltpu.make_async_remote_copy(
            src_ref=down_out.at[piece],
            dst_ref=down_in.at[piece],
            send_sem=down_sems.at[0, piece],
            recv_sem=down_sems.at[1, piece],
            device_id=(following,),
            device_id_type=MESH,
        )

    def up_copy(piece):
        return pltpu.make_async_remote_copy(
            src_ref=up_out.at[piece],
            dst_ref=up_in.at[piece],
            send_sem=up_sems.at[0, piece],
            recv_sem=up_sems.at[1, piece],
            device_id=(preceding,),
            device_id_type=MESH,
        )

    def planes_down_copy(piece):
        return pltpu.make_async_remote_copy(
            src_ref=stack.at[piece, pl.ds(DEPTH + 4, 3), pl.ds(0, SLOTS), :],
            dst_ref=from_prev.at[piece, pl.ds(1, 3)],
            send_sem=planes_down_sems.at[0, piece],
            recv_sem=planes_down_sems.at[1, piece],
            device_id=(following,),
            device_id_type=MESH,
        )

    def planes_up_copy(piece):
        return pltpu.make_async_remote_copy(
            src_ref=stack.at[piece, pl.ds(0, 3), pl.ds(0, SLOTS), :],
            dst_ref=from_next.at[piece, pl.ds(0, 3)],
            send_sem=planes_up_sems.at[0, piece],
            recv_sem=planes_up_sems.at[1, piece],
            device_id=(preceding,),
            device_id_type=MESH,
        )

    def plane_up_copy(piece):
        return pltpu.make_async_remote_copy(
            src_ref=stack.at[piece, 3, pl.ds(0, SLOTS), :],
            dst_ref=from_next.at[piece, 3],
            send_sem=plane_sems.at[0, piece],
            recv_sem=plane_sems.at[1, piece],
            device_id=(preceding,),
            device_id_type=MESH,
        )

    def plane_down_copy(piece):
        return pltpu.make_async_remote_copy(
            src_ref=stack.at[piece, DEPTH + 3, pl.ds(0, SLOTS), :],
            dst_ref=from_prev.at[piece, 0],
            send_sem=plane_sems.at[0, piece],
            recv_sem=plane_sems.at[1, piece],
            device_id=(following,),
            device_id_type=MESH,
        )

    def place_piece(piece, carry):
        raw_copy(piece).wait()
        dens[...] = jnp.zeros_like(dens)

        def place_group(group, carry):
            slots = pl.ds(pl.multiple_of(group * GROUP, GROUP), GROUP)
            source = raw[piece, pl.ds(pl.multiple_of(group * GROUP * DEPTH, GROUP * DEPTH), GROUP * DEPTH), :]
            placed = jnp.dot(selector[group], source, preferred_element_type=F32)
            placed = placed.reshape(PLANES, GROUP, width)
            stack[piece, :, slots, :] = placed.astype(BF16)
            weight = jnp.concatenate([wide_weights[slots, :]] * (width // SLOTS), axis=1)
            terms = placed * placed * weight[None]
            dens[...] += terms[:, :DEPTH] + terms[:, DEPTH:]
            return carry

        lax.fori_loop(0, GROUPS, place_group, 0)
        down_out[piece] = jnp.zeros_like(down_out[piece])
        down_out[piece, : DEPTH - 1] = jnp.sum(dens[DEPTH:], axis=1)
        up_out[piece, 0] = nucleus[:, points(piece)] + jnp.sum(dens[:DEPTH], axis=1)
        up_out[piece, 1] = applied[:, points(piece)]
        down_copy(piece).start()
        up_copy(piece).start()
        planes_down_copy(piece).start()
        planes_up_copy(piece).start()

        @pl.when(piece < PIECES // 2)
        def _():
            plane_up_copy(piece).start()

        @pl.when(piece >= PIECES // 2)
        def _():
            plane_down_copy(piece).start()

        return carry

    lax.fori_loop(0, PIECES, place_piece, 0)

    def own_piece(piece, carry):
        down_copy(piece).wait()
        up_copy(piece).wait()
        density = up_out[piece, 0] + down_in[piece]
        pot[piece, :DEPTH] = up_out[piece, 1] - 0.9847 * cube_root(density)
        pot[piece, DEPTH:] = up_in[piece, 1] - 0.9847 * cube_root(up_in[piece, 0] + down_out[piece])
        for plane in range(PLANES):
            phi = stack[piece, plane, :SLOTS, :]
            stack[piece, plane, SLOTS:, :] = (phi.astype(F32) * pot[piece, plane : plane + 1, :]).astype(BF16)
        return carry

    lax.fori_loop(0, PIECES, own_piece, 0)
    part[...] = jnp.zeros_like(part)

    def cross_piece(piece, carry):
        planes_up_copy(piece).wait()
        planes_down_copy(piece).wait()
        total = part[0]
        for shared in range(3):
            total += dot_nt(from_next[piece, shared], stack[piece, DEPTH + shared])
        part[0] = total
        total = part[1]
        for shared in range(4, 7):
            total += dot_nt(from_prev[piece, shared - 3], stack[piece, shared])
        part[1] = total

        @pl.when(piece < PIECES // 2)
        def _():
            plane_up_copy(piece).wait()
            part[0] += dot_nt(from_next[piece, 3], stack[piece, DEPTH + 3])

        @pl.when(piece >= PIECES // 2)
        def _():
            plane_down_copy(piece).wait()
            part[1] += dot_nt(from_prev[piece, 0], stack[piece, 3])

        return carry

    lax.fori_loop(0, PIECES, cross_piece, 0)

    def part_copy(side, target):
        return pltpu.make_async_remote_copy(
            src_ref=part.at[side],
            dst_ref=part_in.at[side],
            send_sem=part_sems.at[0, side],
            recv_sem=part_sems.at[1, side],
            device_id=(target,),
            device_id_type=MESH,
        )

    to_next = part_copy(0, following)
    to_prev = part_copy(1, preceding)
    to_next.start()
    to_prev.start()
    to_next.wait()
    to_prev.wait()
    side[0, :SLOTS] = part[0, :, :SLOTS].T + part_in[1, :, :SLOTS]
    side[0, SLOTS:] = part[0, :, SLOTS:].T + part_in[1, :, SLOTS:]
    side[1, :SLOTS] = part[1, :, :SLOTS].T + part_in[0, :, :SLOTS]
    side[1, SLOTS:] = part[1, :, SLOTS:].T + part_in[0, :, SLOTS:]
    side_copy = pltpu.make_async_copy(side, side_out, out_sem)
    side_copy.start()
    side_copy.wait()


def full_call(
    basis_wavefunctions,
    filling_weights,
    living_per_unit,
    starting_sheets,
    nucleus_charge,
    applied_field,
):
    slots, depth, points = basis_wavefunctions.shape
    count = lax.axis_size("func")
    width = points // PIECES
    vmem = pl.BlockSpec(memory_space=pltpu.VMEM)
    anywhere = pl.BlockSpec(memory_space=pl.ANY)
    pair = pltpu.SemaphoreType.DMA((2, PIECES))
    return pl.pallas_call(
        functools.partial(full_kernel, count),
        out_shape=jax.ShapeDtypeStruct((2, 2 * slots, slots), F32),
        in_specs=[
            anywhere,
            vmem,
            pl.BlockSpec(memory_space=pltpu.SMEM),
            vmem,
            vmem,
            vmem,
        ],
        out_specs=anywhere,
        scratch_shapes=[
            pltpu.VMEM((PIECES, slots * depth, width), BF16),
            pltpu.VMEM((GROUPS, PLANES * GROUP, slots), BF16),
            pltpu.VMEM((slots, slots), F32),
            pltpu.VMEM((PIECES, PLANES, 2 * slots, width), BF16),
            pltpu.VMEM((PIECES, 4, slots, width), BF16),
            pltpu.VMEM((PIECES, 4, slots, width), BF16),
            pltpu.VMEM((PLANES, DEPTH, width), F32),
            pltpu.VMEM((PIECES, 2 * DEPTH, width), F32),
            pltpu.VMEM((PIECES, 2, DEPTH, width), F32),
            pltpu.VMEM((PIECES, 2, DEPTH, width), F32),
            pltpu.VMEM((PIECES, DEPTH, width), F32),
            pltpu.VMEM((PIECES, DEPTH, width), F32),
            pltpu.VMEM((2, slots, 2 * slots), F32),
            pltpu.VMEM((2, slots, 2 * slots), F32),
            pltpu.VMEM((2, 2 * slots, slots), F32),
            pltpu.SemaphoreType.DMA((PIECES,)),
            pair,
            pair,
            pair,
            pair,
            pair,
            pltpu.SemaphoreType.DMA((2, 2)),
            pltpu.SemaphoreType.DMA,
        ],
        compiler_params=pltpu.CompilerParams(
            collective_id=1, has_side_effects=True, vmem_limit_bytes=56 * 2**20
        ),
        cost_estimate=pl.CostEstimate(
            flops=4 * 10**9, bytes_accessed=5 * 2**20, transcendentals=2**16
        ),
    )(
        basis_wavefunctions.reshape(slots * depth, points),
        filling_weights.reshape(1, slots),
        living_per_unit,
        starting_sheets.reshape(count, slots),
        nucleus_charge,
        applied_field,
    )


def per_device(
    basis_wavefunctions,
    filling_weights,
    living_per_unit,
    starting_sheets,
    nucleus_charge,
    applied_field,
):
    slots, depth, points = basis_wavefunctions.shape
    count = lax.axis_size("func")
    width = points // PIECES
    anywhere = pl.BlockSpec(memory_space=pl.ANY)
    pair = pltpu.SemaphoreType.DMA((2, PIECES))
    rho, own, side, part_in, back, over = pl.pallas_call(
        functools.partial(packed_kernel, count),
        out_shape=(
            jax.ShapeDtypeStruct((depth, points), F32),
            jax.ShapeDtypeStruct((slots, 2 * slots), F32),
            jax.ShapeDtypeStruct((2, 2 * slots, slots), F32),
            jax.ShapeDtypeStruct((2, max(PARTS), 2 * slots), F32),
            jax.ShapeDtypeStruct((2, slots, slots), BF16),
            jax.ShapeDtypeStruct((1,), F32),
        ),
        in_specs=[anywhere] * 6,
        out_specs=(anywhere,) * 5 + (pl.BlockSpec(memory_space=pltpu.SMEM),),
        scratch_shapes=[
            pltpu.VMEM((PIECES, slots * depth, width), BF16),
            pltpu.VMEM((1, slots), F32),
            pltpu.VMEM((1, count), jnp.int32),
            pltpu.VMEM((count, slots), jnp.int32),
            pltpu.VMEM((depth, points), F32),
            pltpu.VMEM((depth, points), F32),
            pltpu.VMEM((count, slots), F32),
            pltpu.VMEM((GROUPS, PLANES * GROUP, slots), BF16),
            pltpu.VMEM((slots, slots), F32),
            pltpu.VMEM((2, slots, slots), BF16),
            pltpu.VMEM((2, slots, slots), BF16),
            pltpu.VMEM((PIECES, PLANES, 2 * slots, width), BF16),
            pltpu.VMEM((PIECES, MANY, width), BF16),
            pltpu.VMEM((PIECES, MANY, width), BF16),
            pltpu.VMEM((PIECES, MANY, width), BF16),
            pltpu.VMEM((PIECES, MANY, width), BF16),
            pltpu.VMEM((PIECES, 2 * DEPTH, width), F32),
            pltpu.VMEM((depth, points), F32),
            pltpu.VMEM((PIECES, DEPTH, width), F32),
            pltpu.VMEM((PIECES, 2 * DEPTH, width), BF16),
            pltpu.VMEM((PIECES, 2 * DEPTH, width), BF16),
            pltpu.VMEM((PIECES, DEPTH, width), F32),
            pltpu.VMEM((PIECES, DEPTH, width), F32),
            pltpu.VMEM((slots, 2 * slots), F32),
            pltpu.VMEM((2, slots, 2 * slots), F32),
            pltpu.VMEM((2, 2 * slots, slots), F32),
            pltpu.SemaphoreType.DMA((PIECES,)),
            pltpu.SemaphoreType.DMA((5,)),
            pair,
            pair,
            pair,
            pair,
            pltpu.SemaphoreType.DMA((2, 2)),
            pltpu.SemaphoreType.DMA((4,)),
        ],
        compiler_params=pltpu.CompilerParams(
            collective_id=0, has_side_effects=True, vmem_limit_bytes=56 * 2**20
        ),
        cost_estimate=pl.CostEstimate(
            flops=4 * 10**9, bytes_accessed=5 * 2**20, transcendentals=2**16
        ),
    )(
        basis_wavefunctions.reshape(slots * depth, points),
        filling_weights.reshape(1, slots),
        living_per_unit.reshape(1, count),
        starting_sheets.reshape(count, slots),
        nucleus_charge,
        applied_field,
    )

    def as_sent():
        return side, part_in, rho, own, back

    def in_full():
        whole = full_call(
            basis_wavefunctions,
            filling_weights,
            living_per_unit,
            starting_sheets,
            nucleus_charge,
            applied_field,
        )
        return whole, jnp.zeros_like(part_in), rho, own, back

    given = lax.cond(over[0] > 0.0, in_full, as_sent)
    return tuple(
        pl.pallas_call(
            functools.partial(finish_kernel, 1.0 / (depth * points)),
            out_shape=(
                jax.ShapeDtypeStruct((depth, points), F32),
                jax.ShapeDtypeStruct((slots, 3 * slots), F32),
                jax.ShapeDtypeStruct((slots, 3 * slots), F32),
            ),
        )(*given)
    )


def solution(mesh):
    return jax.shard_map(
        per_device,
        mesh=mesh,
        in_specs=(P("func", None, None), P("func"), P(), P(), P("func", None), P("func", None)),
        out_specs=(P("func", None), P("func", None), P("func", None)),
        check_vma=False,
    )
```
